256 devices in a mesh: tm: 16 (over z, core), height: 8 (over x, y_hi), batch: 2 (over y_lo).
Axes of the slice: x: 4, y: 4 (y_hi: 2, y_lo: 2; y = y_hi * 2 + y_lo), z: 8, core: 2. Of those that a mesh axis runs over, the one named last changes fastest.
Arguments:
- features: bfloat16 [2, 64, 64, 64, 256], P('batch', None, 'tm', 'height'), may hold values from -6 to 6
- cotangent: bfloat16 [2, 64, 64, 64, 256], P('batch', None, 'tm', 'height'), may hold values from -6 to 6
- w_spatial: bfloat16 [3, 3, 64, 64], replicated, may hold values from -0.25 to 0.25
- w_first: bfloat16 [3, 64, 64], replicated, may hold values from -0.4375 to 0.4375
- w_second: bfloat16 [3, 64, 64], replicated, may hold values from -0.4375 to 0.4375
Outputs:
- input_grad: bfloat16 [2, 64, 64, 64, 256], P('batch', None, 'tm', 'height')
- grad_spatial: float32 [3, 3, 64, 64], replicated
- grad_first: float32 [3, 64, 64], replicated
- grad_second: float32 [3, 64, 64], replicated
The draws below stay inside these ranges and needn't reach their ends.
All inputs are finite; a program needn't handle non-finite values.
Results may differ from the reference program's by a relative error of at most 0.0058.
Values may be sent and summed in bfloat16 or wider, within the bound.
A program may use at most 64 MiB of HBM per device.

```python
import math
import jax
import jax.numpy as jnp
from jax import lax

CH = 64
WIDTH = 256
FRAMES = 64
ROWS = 64
CLIPS = 2


def block_levels(own_key, extent, split, least, high):
    loudness = 1.0
    for dim, shards_of in split:
        draws = jax.random.uniform(jax.random.fold_in(jax.random.fold_in(own_key, 6), dim), (shards_of,), jnp.float32, least / len(split), high / len(split))
        loudness = loudness * jnp.repeat(jnp.exp(draws), extent[dim] // shards_of).reshape((-1,) + (1,) * (len(extent) - 1 - dim))
    return loudness


def centred(own_key, dims, spread, most, shards=(), kind=jnp.bfloat16):
    level = block_levels(own_key, dims, shards, -0.22, 0.18) if shards else 1.0
    result = jax.random.normal(own_key, dims, jnp.float32) * spread * level
    return jnp.minimum(jnp.maximum(result, -most), most).astype(kind)


def setup_inputs(seed: int = 0) -> dict:
    key_list = jax.random.split(jax.random.key(seed), 6)
    features = centred(key_list[0], (CLIPS, CH, FRAMES, ROWS, WIDTH), 1.0, 6.0, ((0, 2), (2, 16), (3, 8)))
    cotangent = centred(key_list[1], (CLIPS, CH, FRAMES, ROWS, WIDTH), 1.0, 6.0, ((0, 2), (2, 16), (3, 8)))
    w_spatial = centred(key_list[2], (3, 3, CH, CH), (9 * CH) ** -0.5, 0.25)
    w_first = centred(key_list[3], (3, CH, CH), (3 * CH) ** -0.5, 0.4375)
    w_second = centred(key_list[4], (3, CH, CH), (3 * CH) ** -0.5, 0.4375)
    return {"features": features, "cotangent": cotangent, "w_spatial": w_spatial, "w_first": w_first, "w_second": w_second}


def activate(value):
    return 0.2 * value + 0.8 * value * jax.nn.sigmoid(value)

def derivative(value):
    sig = jax.nn.sigmoid(value)
    return 0.2 + 0.8 * sig * (1.0 + value * (1.0 - sig))

def shift_cols(value, step):
    if step == 0:
        return value
    zeros = jnp.zeros(value.shape[:-1] + (abs(step),), value.dtype)
    if step > 0:
        return jnp.concatenate([value[..., step:], zeros], axis=-1)
    return jnp.concatenate([zeros, value[..., :step]], axis=-1)

def pad_rows(value):
    return jnp.pad(value, ((0, 0), (0, 0), (1, 1), (0, 0)))

def reference(features, cotangent, w_spatial, w_first, w_second):
    frames_first = jnp.moveaxis(features, 2, 0)
    cot_first = jnp.moveaxis(cotangent, 2, 0)
    nframes = frames_first.shape[0]
    nrows = frames_first.shape[3]
    ws = w_spatial.astype(jnp.float32)
    wa = w_first.astype(jnp.float32)
    wb = w_second.astype(jnp.float32)
    order = jnp.arange(nframes, dtype=jnp.int32)

    def spatial(frame):
        padded = pad_rows(frame.astype(jnp.float32))
        total = jnp.zeros(frame.shape, jnp.float32)
        for j in range(3):
            moved = shift_cols(padded, j - 1)
            for i in range(3):
                total = total + jnp.einsum('oc,bchw->bohw', ws[i, j], moved[:, :, i:i + nrows])
        return total
    first_pre = lax.map(spatial, frames_first)
    first = activate(first_pre).astype(jnp.bfloat16)

    def temporal(source, weight, dilation):

        def one(index):
            total = jnp.zeros(source.shape[1:], jnp.float32)
            for k in range(3):
                other = source[jnp.mod(index + dilation * (k - 1), nframes)].astype(jnp.float32)
                total = total + jnp.einsum('oc,bchw->bohw', weight[k], other)
            return total
        return lax.map(one, order)

    def transposed(source, weight, dilation):

        def one(index):
            total = jnp.zeros(source.shape[1:], jnp.float32)
            for k in range(3):
                other = source[jnp.mod(index - dilation * (k - 1), nframes)].astype(jnp.float32)
                total = total + jnp.einsum('oc,bohw->bchw', weight[k], other)
            return total
        return lax.map(one, order)
    second_pre = temporal(first, wa, 1)
    second = activate(second_pre).astype(jnp.bfloat16)
    back_second = (transposed(cot_first, wb, 2) * derivative(second_pre)).astype(jnp.bfloat16)
    back_first = (transposed(back_second, wa, 1) * derivative(first_pre)).astype(jnp.bfloat16)

    def kernel_grad(grads, source, dilation):

        def step(carry, index):
            here = grads[index].astype(jnp.float32)
            terms = []
            for k in range(3):
                other = source[jnp.mod(index + dilation * (k - 1), nframes)].astype(jnp.float32)
                terms.append(jnp.einsum('bohw,bchw->oc', here, other))
            return (carry + jnp.stack(terms), None)
        start = jnp.zeros((3, grads.shape[2], source.shape[2]), jnp.float32)
        return lax.scan(step, start, order)[0]

    def spatial_grad(carry, index):
        here = back_first[index].astype(jnp.float32)
        padded = pad_rows(frames_first[index].astype(jnp.float32))
        rows_out = []
        for i in range(3):
            cols_out = []
            for j in range(3):
                moved = shift_cols(padded, j - 1)[:, :, i:i + nrows]
                cols_out.append(jnp.einsum('bohw,bchw->oc', here, moved))
            rows_out.append(jnp.stack(cols_out))
        return (carry + jnp.stack(rows_out), None)
    gsp = lax.scan(spatial_grad, jnp.zeros(w_spatial.shape, jnp.float32), order)[0]
    gfirst = kernel_grad(back_second, first, 1)
    gsecond = kernel_grad(cot_first, second, 2)

    def input_frame(frame):
        padded = pad_rows(frame.astype(jnp.float32))
        total = jnp.zeros(frame.shape, jnp.float32)
        for i in range(3):
            for j in range(3):
                moved = shift_cols(padded[:, :, 2 - i:2 - i + nrows], 1 - j)
                total = total + jnp.einsum('oc,bohw->bchw', ws[i, j], moved)
        return total.astype(jnp.bfloat16)
    input_grad = jnp.moveaxis(lax.map(input_frame, back_first), 0, 2)
    count = features.shape[0] * features.shape[2] * features.shape[3] * features.shape[4]
    scale = 1.0 / math.sqrt(count)
    return (input_grad, gsp * scale, gfirst * scale, gsecond * scale)
```

```python
import functools
import math

import jax
import jax.numpy as jnp
from jax import lax
from jax.experimental import pallas as pl
from jax.experimental.pallas import tpu as pltpu
from jax.sharding import PartitionSpec as P

BF16 = jnp.bfloat16
F32 = jnp.float32
MESH = pl.DeviceIdType.MESH
CH = 64
AXES = ("tm", "height", "batch")


def dot(left, right):
    return jnp.dot(left, right, preferred_element_type=F32)


def dot_nt(left, right):
    return lax.dot_general(left, right, (((1,), (1,)), ((), ())), preferred_element_type=F32)


def gate(value):
    t = jnp.tanh(0.5 * value)
    g = 0.6 + 0.4 * t
    return value * g, g + 0.2 * value * (1.0 - t * t)


def kernel(
    sizes, scale,
    feat, cot, ws, w1, w2,
    out, gs, g1, g2,
    raw_f, raw_c, raw_o, X, FI, D1, CT, S2, SE, BS, BF, BFL, BFR, IG,
    WF, WB, W1F, W1B, W2B, PIN, POUT,
    acc1, acc2, acc3, pack1, pack2,
    a1s, a1r, b1r, c1r, a2s, a2r, b2r, c2r,
    sem_in, sem_out, xs, xr, cs, cr, fs, fr, bs, br, rs, rr, ars, arr,
):
    ntm, nheight, nbatch = sizes
    nxy = nheight * nbatch
    nf, nr, width = raw_f.shape[0], raw_f.shape[2], raw_f.shape[3]
    t = lax.axis_index("tm")
    hh = lax.axis_index("height")
    b = lax.axis_index("batch")
    me = hh * nbatch + b
    before = (lax.rem(t + ntm - 1, ntm), hh, b)
    after = (lax.rem(t + 1, ntm), hh, b)
    above = (t, hh - 1, b)
    below = (t, hh + 1, b)
    has_above = hh > 0
    has_below = hh < nheight - 1

    def xy_device(g):
        return (t, g // nbatch, lax.rem(g, nbatch))

    def tm_device(s):
        return (s, hh, b)

    barrier = pltpu.get_barrier_semaphore()

    def greet_xy(d, _):
        pl.semaphore_signal(barrier, inc=1, device_id=xy_device(lax.rem(me + d, nxy)), device_id_type=MESH)
        return 0

    def greet_tm(d, _):
        pl.semaphore_signal(barrier, inc=1, device_id=tm_device(lax.rem(t + d, ntm)), device_id_type=MESH)
        return 0

    loads_f = [pltpu.make_async_copy(feat.at[:, f], raw_f.at[f], sem_in.at[f]) for f in range(nf)]
    loads_c = [pltpu.make_async_copy(cot.at[:, f], raw_c.at[f], sem_in.at[nf + f]) for f in range(nf)]
    for copy in loads_f + loads_c:
        copy.start()
    lax.fori_loop(1, nxy, greet_xy, 0)
    lax.fori_loop(1, ntm, greet_tm, 0)

    row = lax.broadcasted_iota(jnp.int32, (CH, 3 * CH), 0)
    col = lax.broadcasted_iota(jnp.int32, (CH, 3 * CH), 1)
    place = [jnp.where(col == row + CH * i, 1.0, 0.0).astype(BF16) for i in range(3)]
    eye = jnp.where(row[:, :CH] == col[:, :CH], 1.0, 0.0).astype(BF16)
    half = CH // 2
    prow = lax.broadcasted_iota(jnp.int32, (half * nr, half * nr), 0)
    pcol = lax.broadcasted_iota(jnp.int32, (half * nr, half * nr), 1)
    PIN[...] = jnp.where(pcol == lax.rem(prow, half) * nr + prow // half, 1.0, 0.0).astype(BF16)
    POUT[...] = jnp.where(prow == lax.rem(pcol, half) * nr + pcol // half, 1.0, 0.0).astype(BF16)
    for j in range(3):
        ahead = dot(ws[0, j], place[0]) + dot(ws[1, j], place[1]) + dot(ws[2, j], place[2])
        WF[pl.ds(CH * j, CH), :] = ahead.astype(BF16)
        turned = dot_nt(eye, jnp.concatenate([ws[2, j], ws[1, j], ws[0, j]], axis=0))
        WB[pl.ds(CH * j, CH), :] = turned.astype(BF16)
    W1F[...] = (dot(w1[0], place[0]) + dot(w1[1], place[1]) + dot(w1[2], place[2])).astype(BF16)
    W1B[...] = dot_nt(eye, jnp.concatenate([w1[2], w1[1], w1[0]], axis=0)).astype(BF16)
    W2B[...] = dot_nt(eye, jnp.concatenate([w2[2], w2[1], w2[0]], axis=0)).astype(BF16)

    edge = jnp.zeros((nf, CH, width), BF16)

    @pl.when(jnp.logical_not(has_above))
    def _():
        X[:, 0] = edge
        BF[:, 0] = edge

    @pl.when(jnp.logical_not(has_below))
    def _():
        X[:, nr + 1] = edge
        BF[:, nr + 1] = edge

    lane = lax.broadcasted_iota(jnp.int32, (CH, width), 1)

    def from_left(value):
        return jnp.where(lane == 0, 0.0, pltpu.roll(value, 1, 1))

    def from_right(value):
        return jnp.where(lane == width - 1, 0.0, pltpu.roll(value, width - 1, 1))

    def to_rows(raw, part):
        block = raw[pl.ds(half * part, half)].astype(F32).reshape(half * nr, width).astype(BF16)
        return dot(PIN[...], block).astype(BF16).reshape(nr, half, width)

    for f in range(nf):
        loads_f[f].wait()
        for part in range(2):
            X[f, pl.ds(1, nr), pl.ds(half * part, half), :] = to_rows(raw_f.at[f], part)

    pl.semaphore_wait(barrier, nxy - 1 + ntm - 1)

    def remote(src, dst, send, recv, device):
        return pltpu.make_async_remote_copy(
            src_ref=src, dst_ref=dst, send_sem=send, recv_sem=recv, device_id=device, device_id_type=MESH
        )

    x_up = remote(X.at[:, 1], X.at[:, nr + 1], xs.at[0], xr.at[0], above)
    x_down = remote(X.at[:, nr], X.at[:, 0], xs.at[1], xr.at[1], below)

    @pl.when(has_above)
    def _():
        x_up.start()

    @pl.when(has_below)
    def _():
        x_down.start()

    for f in range(nf):
        loads_c[f].wait()
        for part in range(2):
            CT[:, f % 2, f // 2 + 1, pl.ds(half * part, half), :] = to_rows(raw_c.at[f], part)
    c_back = remote(CT.at[:, :, 1], CT.at[:, :, 3], cs.at[0], cr.at[0], before)
    c_fore = remote(CT.at[:, :, 2], CT.at[:, :, 0], cs.at[1], cr.at[1], after)
    c_back.start()
    c_fore.start()

    def conv_row(f, h):
        z = dot(WF[...], X[f, pl.ds(h, 3)].reshape(3 * CH, width))
        value = z[CH : 2 * CH] + from_left(z[:CH]) + from_right(z[2 * CH :])
        act, der = gate(value)
        FI[h, f + 1] = act.astype(BF16)
        D1[f, h] = der

    def conv_inner(f, _):
        for h in range(1, nr - 1):
            conv_row(f, h)
        return 0

    lax.fori_loop(0, nf, conv_inner, 0)

    @pl.when(has_above)
    def _():
        x_up.wait_send()
        x_down.wait_recv()

    @pl.when(has_below)
    def _():
        x_down.wait_send()
        x_up.wait_recv()

    for f in (0, nf - 1):
        conv_row(f, 0)
        conv_row(f, nr - 1)
    f_back = remote(FI.at[:, 1], FI.at[:, nf + 1], fs.at[0], fr.at[0], before)
    f_fore = remote(FI.at[:, nf], FI.at[:, 0], fs.at[1], fr.at[1], after)
    f_back.start()
    f_fore.start()
    for f in range(1, nf - 1):
        conv_row(f, 0)
        conv_row(f, nr - 1)

    c_back.wait_send()
    c_fore.wait_send()
    c_back.wait_recv()
    c_fore.wait_recv()

    def back_two(h, _):
        for p in range(2):
            for q in range(2):
                S2[h, p, q] = dot(W2B[...], CT[h, p, pl.ds(q, 3)].reshape(3 * CH, width))
        return 0

    lax.fori_loop(0, nr, back_two, 0)

    def second_frame(f, h):
        value = dot(W1F[...], FI[h, pl.ds(f, 3)].reshape(3 * CH, width))
        act, der = gate(value)
        SE[h, f % 2, f // 2] = act.astype(BF16)
        BS[h, f + 1] = (S2[h, f % 2, f // 2] * der).astype(BF16)

    def second_inner(h, _):
        for f in range(1, nf - 1):
            second_frame(f, h)
        return 0

    def second_outer(h, _):
        second_frame(0, h)
        second_frame(nf - 1, h)
        return 0

    lax.fori_loop(0, nr, second_inner, 0)
    f_back.wait_send()
    f_fore.wait_send()
    f_back.wait_recv()
    f_fore.wait_recv()
    lax.fori_loop(0, nr, second_outer, 0)
    b_back = remote(BS.at[:, 1], BS.at[:, nf + 1], bs.at[0], br.at[0], before)
    b_fore = remote(BS.at[:, nf], BS.at[:, 0], bs.at[1], br.at[1], after)
    b_back.start()
    b_fore.start()

    acc1[...] = jnp.zeros_like(acc1)
    acc2[...] = jnp.zeros_like(acc2)

    def temporal_grads(h, _):
        total1 = acc1[...]
        total2 = acc2[...]
        for f in range(0, nf, 2):
            total1 += dot_nt(
                BS[h, pl.ds(f + 1, 2)].reshape(2 * CH, width), FI[h, pl.ds(f, 4)].reshape(4 * CH, width)
            )
        for p in range(2):
            total2 += dot_nt(CT[h, p].reshape(4 * CH, width), SE[h, p].reshape(2 * CH, width))
        acc1[...] = total1
        acc2[...] = total2
        return 0

    lax.fori_loop(0, nr, temporal_grads, 0)

    low = lax.broadcasted_iota(jnp.int32, (CH, 2 * CH), 1) < CH

    def side_by_side(left, right):
        return jnp.where(low[: left.shape[0]], left, pltpu.roll(right, CH, 1))

    def reduce_scatter(pack, send, recv, which):
        rows = send.shape[1]
        for g in range(nxy):
            send[g] = pack[pl.ds(rows * g, rows), :]
        recv[me] = send[me]

        def one(d, _):
            g = lax.rem(me + d, nxy)
            remote(send.at[g], recv.at[me], ars.at[which], arr.at[which], xy_device(g)).start()
            return 0

        lax.fori_loop(1, nxy, one, 0)

    def await_all(ref, count, sem):
        part = ref.at[pl.ds(0, count)]
        pltpu.make_async_copy(part, part, sem).wait()

    def added(ref):
        total = ref[0]
        for g in range(1, ref.shape[0]):
            total += ref[g]
        return total

    def exchange_tm(send, recv, spread, which):
        await_all(recv, nxy - 1, arr.at[which])
        await_all(send, nxy - 1, ars.at[which])
        spread[t] = added(recv)

        def one(d, _):
            s = lax.rem(t + d, ntm)
            remote(spread.at[t], spread.at[t], ars.at[which + 1], arr.at[which + 1], tm_device(s)).start()
            return 0

        lax.fori_loop(1, ntm, one, 0)

    def gather_xy(spread, gathered, which):
        await_all(spread, ntm - 1, arr.at[which + 1])
        await_all(spread, ntm - 1, ars.at[which + 1])
        gathered[me] = added(spread)

        def one(d, _):
            g = lax.rem(me + d, nxy)
            remote(gathered.at[me], gathered.at[me], ars.at[which + 2], arr.at[which + 2], xy_device(g)).start()
            return 0

        lax.fori_loop(1, nxy, one, 0)

    def unpack(pack, gathered, which):
        await_all(gathered, nxy - 1, arr.at[which + 2])
        await_all(gathered, nxy - 1, ars.at[which + 2])
        rows = gathered.shape[1]
        for g in range(nxy):
            pack[pl.ds(rows * g, rows), :] = gathered[g] * scale

    s1 = acc1[pl.ds(0, CH), :] + pltpu.roll(acc1[pl.ds(CH, CH), :], 3 * CH, 1)
    s2 = acc2[pl.ds(0, 3 * CH), :] + pltpu.roll(acc2[pl.ds(CH, 3 * CH), :], CH, 1)
    pack1[pl.ds(0, CH), :] = s1[:, : 2 * CH]
    pack1[pl.ds(CH, CH), :] = side_by_side(s1[:, 2 * CH :], s2[:CH])
    pack1[pl.ds(2 * CH, CH), :] = side_by_side(s2[CH : 2 * CH], s2[2 * CH :])
    reduce_scatter(pack1, a1s, a1r, 0)

    def back_frame(f, h):
        value = dot(W1B[...], BS[h, pl.ds(f, 3)].reshape(3 * CH, width)) * D1[f, h]
        BF[f, h + 1] = value.astype(BF16)
        BFL[f, h] = from_right(value).astype(BF16)
        BFR[f, h] = from_left(value).astype(BF16)

    def back_inner(h, _):
        for f in range(1, nf - 1):
            back_frame(f, h)
        return 0

    def back_outer(h, _):
        back_frame(0, h)
        back_frame(nf - 1, h)
        return 0

    ups = [
        remote(BF.at[f, 1], BF.at[f, nr + 1], rs.at[f], rr.at[f], above) for f in range(nf)
    ]
    downs = [
        remote(BF.at[f, nr], BF.at[f, 0], rs.at[nf + f], rr.at[nf + f], below) for f in range(nf)
    ]

    def send_rows(frames):
        @pl.when(has_above)
        def _():
            for f in frames:
                ups[f].start()

        @pl.when(has_below)
        def _():
            for f in frames:
                downs[f].start()

    lax.fori_loop(0, nr, back_inner, 0)
    send_rows(range(1, nf - 1))
    b_back.wait_send()
    b_fore.wait_send()
    b_back.wait_recv()
    b_fore.wait_recv()
    lax.fori_loop(0, nr, back_outer, 0)
    send_rows((0, nf - 1))

    exchange_tm(a1s, a1r, b1r, 0)

    acc3[...] = jnp.zeros_like(acc3)

    def spatial_grads(f, _):
        for h in range(0, nr, 2):
            left = jnp.concatenate(
                [
                    BFL[f, pl.ds(h, 2)].reshape(2 * CH, width),
                    BF[f, pl.ds(h + 1, 2)].reshape(2 * CH, width),
                    BFR[f, pl.ds(h, 2)].reshape(2 * CH, width),
                ],
                axis=0,
            )
            acc3[...] += dot_nt(left, X[f, pl.ds(h, 4)].reshape(4 * CH, width))
        return 0

    lax.fori_loop(0, nf, spatial_grads, 0)
    tails = []
    for j in range(3):
        total = acc3[pl.ds(2 * CH * j, CH), :] + pltpu.roll(acc3[pl.ds(2 * CH * j + CH, CH), :], 3 * CH, 1)
        pack2[pl.ds(CH * j, CH), :] = total[:, : 2 * CH]
        tails.append(total[:, 2 * CH :])
    pack2[pl.ds(3 * CH, CH), :] = side_by_side(tails[0], tails[1])
    pack2[pl.ds(4 * CH, half), :] = side_by_side(tails[2][:half], tails[2][half:])
    reduce_scatter(pack2, a2s, a2r, 3)
    gather_xy(b1r, c1r, 0)

    def grad_row(f, h):
        z = dot(WB[...], BF[f, pl.ds(h, 3)].reshape(3 * CH, width))
        value = z[CH : 2 * CH] + from_right(z[:CH]) + from_left(z[2 * CH :])
        IG[f, h] = value.astype(BF16)

    def grad_inner(f, _):
        for h in range(1, nr - 1):
            grad_row(f, h)
        return 0

    lax.fori_loop(0, nf, grad_inner, 0)
    exchange_tm(a2s, a2r, b2r, 3)

    @pl.when(has_above)
    def _():
        for f in range(nf):
            ups[f].wait_send()
            downs[f].wait_recv()

    @pl.when(has_below)
    def _():
        for f in range(nf):
            downs[f].wait_send()
            ups[f].wait_recv()

    stores = [pltpu.make_async_copy(raw_o.at[f], out.at[:, f], sem_out.at[f]) for f in range(nf)]
    for f in range(nf):
        grad_row(f, 0)
        grad_row(f, nr - 1)
        for part in range(2):
            block = IG[f, :, pl.ds(half * part, half), :].reshape(half * nr, width)
            raw_o[f, pl.ds(half * part, half)] = dot(POUT[...], block).reshape(half, nr, width).astype(BF16)
        stores[f].start()

    gather_xy(b2r, c2r, 3)

    unpack(pack1, c1r, 0)
    g1[0] = pack1[pl.ds(0, CH), :CH]
    g1[1] = pack1[pl.ds(0, CH), CH:]
    g1[2] = pack1[pl.ds(CH, CH), :CH]
    g2[2] = pack1[pl.ds(CH, CH), CH:]
    g2[1] = pack1[pl.ds(2 * CH, CH), :CH]
    g2[0] = pack1[pl.ds(2 * CH, CH), CH:]
    unpack(pack2, c2r, 3)
    for j in range(3):
        gs[0, j] = pack2[pl.ds(CH * j, CH), :CH]
        gs[1, j] = pack2[pl.ds(CH * j, CH), CH:]
    gs[2, 0] = pack2[pl.ds(3 * CH, CH), :CH]
    gs[2, 1] = pack2[pl.ds(3 * CH, CH), CH:]
    gs[2, 2, pl.ds(0, half), :] = pack2[pl.ds(4 * CH, half), :CH]
    gs[2, 2, pl.ds(half, half), :] = pack2[pl.ds(4 * CH, half), CH:]
    for f in range(nf):
        stores[f].wait()


def per_device(sizes, features, cotangent, w_spatial, w_first, w_second):
    _, ch, nf, nr, width = features.shape
    ntm, nheight, nbatch = sizes
    nxy = nheight * nbatch
    count = nbatch * nf * ntm * nr * nheight * width
    scale = 1.0 / math.sqrt(count)
    vmem = lambda shape, kind=BF16: pltpu.VMEM(shape, kind)
    rows1, rows2 = 3 * ch // nxy, 9 * ch // 2 // nxy
    dma = pltpu.SemaphoreType.DMA
    scratch = [
        vmem((nf, ch, nr, width)), vmem((nf, ch, nr, width)), vmem((nf, ch, nr, width)),
        vmem((nf, nr + 2, ch, width)),
        vmem((nr, nf + 2, ch, width)),
        vmem((nf, nr, ch, width), F32),
        vmem((nr, 2, nf // 2 + 2, ch, width)),
        vmem((nr, 2, nf // 2, ch, width), F32),
        vmem((nr, 2, nf // 2, ch, width)),
        vmem((nr, nf + 2, ch, width)),
        vmem((nf, nr + 2, ch, width)),
        vmem((nf, nr, ch, width)), vmem((nf, nr, ch, width)), vmem((nf, nr, ch, width)),
        vmem((3 * ch, 3 * ch)), vmem((3 * ch, 3 * ch)),
        vmem((ch, 3 * ch)), vmem((ch, 3 * ch)), vmem((ch, 3 * ch)),
        vmem((ch // 2 * nr, ch // 2 * nr)), vmem((ch // 2 * nr, ch // 2 * nr)),
        vmem((2 * ch, 4 * ch), F32), vmem((4 * ch, 2 * ch), F32), vmem((6 * ch, 4 * ch), F32),
        vmem((3 * ch, 2 * ch), F32), vmem((9 * ch // 2, 2 * ch), F32),
        vmem((nxy, rows1, 2 * ch), F32), vmem((nxy, rows1, 2 * ch), F32),
        vmem((ntm, rows1, 2 * ch), F32), vmem((nxy, rows1, 2 * ch), F32),
        vmem((nxy, rows2, 2 * ch), F32), vmem((nxy, rows2, 2 * ch), F32),
        vmem((ntm, rows2, 2 * ch), F32), vmem((nxy, rows2, 2 * ch), F32),
        dma((2 * nf,)), dma((nf,)),
        dma((2,)), dma((2,)), dma((2,)), dma((2,)), dma((2,)), dma((2,)), dma((2,)), dma((2,)),
        dma((2 * nf,)), dma((2 * nf,)), dma((6,)), dma((6,)),
    ]
    here = pl.BlockSpec(memory_space=pltpu.VMEM)
    anywhere = pl.BlockSpec(memory_space=pl.ANY)
    input_grad, grad_spatial, grad_first, grad_second = pl.pallas_call(
        functools.partial(kernel, sizes, scale),
        out_shape=(
            jax.ShapeDtypeStruct((ch, nf, nr, width), BF16),
            jax.ShapeDtypeStruct((3, 3, ch, ch), F32),
            jax.ShapeDtypeStruct((3, ch, ch), F32),
            jax.ShapeDtypeStruct((3, ch, ch), F32),
        ),
        in_specs=[anywhere, anywhere, here, here, here],
        out_specs=(anywhere, here, here, here),
        scratch_shapes=scratch,
        compiler_params=pltpu.CompilerParams(
            collective_id=0, has_side_effects=True, vmem_limit_bytes=48 * 1024 * 1024
        ),
        name="critic_step",
    )(features[0], cotangent[0], w_spatial, w_first, w_second)
    return input_grad[None], grad_spatial, grad_first, grad_second


def solution(mesh):
    sizes = tuple(mesh.shape[axis] for axis in AXES)
    big = P("batch", None, "tm", "height", None)
    return jax.shard_map(
        functools.partial(per_device, sizes),
        mesh=mesh,
        in_specs=(big, big, P(), P(), P()),
        out_specs=(big, P(), P(), P()),
        check_vma=False,
    )
```

```python
import functools
import math

import jax
import jax.numpy as jnp
from jax import lax
from jax.experimental import pallas as pl
from jax.experimental.pallas import tpu as pltpu
from jax.sharding import PartitionSpec as P

BF16 = jnp.bfloat16
F32 = jnp.float32
MESH = pl.DeviceIdType.MESH
CH = 64
AXES = ("tm", "height", "batch")


def dot(left, right):
    return jnp.dot(left, right, preferred_element_type=F32)


def dot_nt(left, right):
    return lax.dot_general(left, right, (((1,), (1,)), ((), ())), preferred_element_type=F32)


def gate(value):
    t = jnp.tanh(0.5 * value)
    g = 0.6 + 0.4 * t
    return value * g, g + 0.2 * value * (1.0 - t * t)


def finish(packed1, packed2, block, out, gs, g1, g2, gs_v, g1_v, g2_v, sems):
    big = pltpu.make_async_copy(block, out, sems.at[0])
    big.start()
    half = CH // 2
    g1_v[0] = packed1[pl.ds(0, CH), :CH]
    g1_v[1] = packed1[pl.ds(0, CH), CH:]
    g1_v[2] = packed1[pl.ds(CH, CH), :CH]
    g2_v[2] = packed1[pl.ds(CH, CH), CH:]
    g2_v[1] = packed1[pl.ds(2 * CH, CH), :CH]
    g2_v[0] = packed1[pl.ds(2 * CH, CH), CH:]
    for j in range(3):
        gs_v[0, j] = packed2[pl.ds(CH * j, CH), :CH]
        gs_v[1, j] = packed2[pl.ds(CH * j, CH), CH:]
    gs_v[2, 0] = packed2[pl.ds(3 * CH, CH), :CH]
    gs_v[2, 1] = packed2[pl.ds(3 * CH, CH), CH:]
    gs_v[2, 2, pl.ds(0, half), :] = packed2[pl.ds(4 * CH, half), :CH]
    gs_v[2, 2, pl.ds(half, half), :] = packed2[pl.ds(4 * CH, half), CH:]
    small = [
        pltpu.make_async_copy(source, target, sems.at[1 + n])
        for n, (source, target) in enumerate(((gs_v, gs), (g1_v, g1), (g2_v, g2)))
    ]
    for copy in small:
        copy.start()
    for copy in small:
        copy.wait()
    big.wait()


def kernel(
    sizes, scale,
    feat, cot, ws_hbm, w1_hbm, w2_hbm,
    raw_o, out1, out2,
    ws, w1, w2, raw_f, raw_c, X, FI, D1, D2, CT, SE, BS, BF, BFL, BFR, IG,
    WF, WB, W1F, W1B, W1F2, W1B2, W2B, PIN, POUT,
    pack1, pack2,
    a1s, a1r, b1r, c1r, a2s, a2r, b2r, c2r,
    sem_in, sends, recvs, ars, arr,
):
    ntm, nheight, nbatch = sizes
    nxy = nheight * nbatch
    nf, nr, width = raw_f.shape[0], raw_f.shape[2], raw_f.shape[3]
    last = nf - 1
    place_of = {0: 0, last: 1, 1: 2, 2: 3}
    outer, inner = (0, last), (1, 2)
    t = lax.axis_index("tm")
    hh = lax.axis_index("height")
    b = lax.axis_index("batch")
    me = hh * nbatch + b
    before = (lax.rem(t + ntm - 1, ntm), hh, b)
    after = (lax.rem(t + 1, ntm), hh, b)
    above = (t, hh - 1, b)
    below = (t, hh + 1, b)
    has_above = hh > 0
    has_below = hh < nheight - 1

    def xy_device(g):
        return (t, g // nbatch, lax.rem(g, nbatch))

    def tm_device(s):
        return (s, hh, b)

    barrier = pltpu.get_barrier_semaphore()

    def greet_xy(d, _):
        pl.semaphore_signal(barrier, inc=1, device_id=xy_device(lax.rem(me + d, nxy)), device_id_type=MESH)
        return 0

    def greet_tm(d, _):
        pl.semaphore_signal(barrier, inc=1, device_id=tm_device(lax.rem(t + d, ntm)), device_id_type=MESH)
        return 0

    loads_w = [
        pltpu.make_async_copy(source, target, sem_in.at[2 * nf + n])
        for n, (source, target) in enumerate(((ws_hbm, ws), (w1_hbm, w1), (w2_hbm, w2)))
    ]
    loads_f = [pltpu.make_async_copy(feat.at[:, f], raw_f.at[f], sem_in.at[f]) for f in range(nf)]
    loads_c = [pltpu.make_async_copy(cot.at[:, f], raw_c.at[f], sem_in.at[nf + f]) for f in range(nf)]
    for copy in loads_w + loads_f + loads_c:
        copy.start()
    lax.fori_loop(1, nxy, greet_xy, 0)
    lax.fori_loop(1, ntm, greet_tm, 0)

    row = lax.broadcasted_iota(jnp.int32, (CH, 4 * CH), 0)
    col = lax.broadcasted_iota(jnp.int32, (CH, 4 * CH), 1)
    place = [jnp.where(col == row + CH * i, 1.0, 0.0).astype(BF16) for i in range(4)]
    eye = place[0][:, :CH]
    half = CH // 2
    prow = lax.broadcasted_iota(jnp.int32, (half * nr, half * nr), 0)
    pcol = lax.broadcasted_iota(jnp.int32, (half * nr, half * nr), 1)
    PIN[...] = jnp.where(pcol == lax.rem(prow, half) * nr + prow // half, 1.0, 0.0).astype(BF16)
    POUT[...] = jnp.where(prow == lax.rem(pcol, half) * nr + pcol // half, 1.0, 0.0).astype(BF16)
    edge = jnp.zeros((nf, CH, width), BF16)

    @pl.when(jnp.logical_not(has_above))
    def _():
        X[:, 0] = edge
        BF[:, 0] = edge

    @pl.when(jnp.logical_not(has_below))
    def _():
        X[:, nr + 1] = edge
        BF[:, nr + 1] = edge

    def side(parts, at):
        total = dot(parts[0], place[at])
        for i in range(1, len(parts)):
            total += dot(parts[i], place[at + i])
        return total.astype(BF16)

    def turned(parts):
        return dot_nt(eye, jnp.concatenate(parts, axis=0)).astype(BF16)

    for copy in loads_w:
        copy.wait()
    for j in range(3):
        WF[pl.ds(CH * j, CH), :] = side([ws[0, j], ws[1, j], ws[2, j]], 0)[:, : 3 * CH]
        WB[pl.ds(CH * j, CH), :] = turned([ws[2, j], ws[1, j], ws[0, j]])
    none = jnp.zeros((CH, CH), BF16)
    W1F[...] = side([w1[0], w1[1], w1[2]], 0)[:, : 3 * CH]
    W1B[...] = turned([w1[2], w1[1], w1[0]])
    W2B[...] = turned([w2[2], w2[1], w2[0]])
    for a in range(2):
        W1F2[pl.ds(CH * a, CH), :] = side([w1[0], w1[1], w1[2]], a)
        W1B2[pl.ds(CH * a, CH), :] = turned([none] * a + [w1[2], w1[1], w1[0]] + [none] * (1 - a))

    lane = lax.broadcasted_iota(jnp.int32, (CH, width), 1)

    def from_left(value):
        return jnp.where(lane == 0, 0.0, pltpu.roll(value, 1, 1))

    def from_right(value):
        return jnp.where(lane == width - 1, 0.0, pltpu.roll(value, width - 1, 1))

    def to_rows(raw, part):
        block = raw[pl.ds(half * part, half)].astype(F32).reshape(half * nr, width).astype(BF16)
        return dot(PIN[...], block).astype(BF16).reshape(nr, half, width)

    def conv_row(at, f, h, s):
        z = dot(WF[...], X[at, pl.ds(h, 3)].reshape(3 * CH, width))
        value = z[CH : 2 * CH] + from_left(z[:CH]) + from_right(z[2 * CH :])
        act, der = gate(value)
        FI[s, f + 1] = act.astype(BF16)
        D1[at, h] = der

    for f in outer + inner:
        loads_f[f].wait()
        for part in range(2):
            X[place_of[f], pl.ds(1, nr), pl.ds(half * part, half), :] = to_rows(raw_f.at[f], part)
        for h in range(1, nr - 1):
            conv_row(place_of[f], f, h, h + 1)
    for f in range(nf):
        loads_c[f].wait()
        for part in range(2):
            lanes = pl.ds(half * part, half)
            block = to_rows(raw_c.at[f], part)
            CT[0, f % 2, f // 2 + 1, lanes, :] = block[0]
            CT[1, f % 2, f // 2 + 1, lanes, :] = block[nr - 1]
            CT[pl.ds(2, nr - 2), f % 2, f // 2 + 1, lanes, :] = block[1 : nr - 1]

    pl.semaphore_wait(barrier, nxy - 1 + ntm - 1)

    used = [0]

    def remote(src, dst, device):
        n = used[0]
        used[0] += 1
        return pltpu.make_async_remote_copy(
            src_ref=src, dst_ref=dst, send_sem=sends.at[n], recv_sem=recvs.at[n],
            device_id=device, device_id_type=MESH,
        )

    class Rows:
        def __init__(self, array, frames):
            self.up = remote(array.at[frames, 1], array.at[frames, nr + 1], above)
            self.down = remote(array.at[frames, nr], array.at[frames, 0], below)

        def start(self):
            pl.when(has_above)(self.up.start)
            pl.when(has_below)(self.down.start)

        def wait(self):
            @pl.when(has_above)
            def _():
                self.up.wait_send()
                self.down.wait_recv()

            @pl.when(has_below)
            def _():
                self.down.wait_send()
                self.up.wait_recv()

    class Frames:
        def __init__(self, back_src, back_dst, fore_src, fore_dst):
            self.both = (remote(back_src, back_dst, before), remote(fore_src, fore_dst, after))

        def start(self):
            for copy in self.both:
                copy.start()

        def wait(self):
            for copy in self.both:
                copy.wait_send()
                copy.wait_recv()

    def outer_frames(array, rows):
        return Frames(array.at[rows, 1], array.at[rows, nf + 1], array.at[rows, nf], array.at[rows, 0])

    edges, middle = pl.ds(0, 2), pl.ds(2, nr - 2)
    first_two, second_two = pl.ds(0, 2), pl.ds(2, 2)
    x_outer, x_inner = Rows(X, first_two), Rows(X, second_two)
    first_middle, first_edges = outer_frames(FI, middle), outer_frames(FI, edges)
    cot_far = Frames(CT.at[:, 1, 1], CT.at[:, 1, 3], CT.at[:, 0, 2], CT.at[:, 0, 0])
    cot_near = Frames(CT.at[:, 0, 1], CT.at[:, 0, 3], CT.at[:, 1, 2], CT.at[:, 1, 0])
    back_middle, back_edges = outer_frames(BS, middle), outer_frames(BS, edges)
    rows_inner, rows_outer = Rows(BF, second_two), Rows(BF, first_two)

    x_outer.start()
    first_middle.start()
    cot_far.start()
    x_inner.start()

    def keep_second(f, s, value):
        act, der = gate(value)
        SE[s, f % 2, f // 2] = act.astype(BF16)
        D2[s, f] = der

    def second_inner(s):
        z = dot(W1F2[...], FI[s, pl.ds(1, 4)].reshape(4 * CH, width))
        keep_second(1, s, z[:CH])
        keep_second(2, s, z[CH:])

    def second_outer(s):
        for f in outer:
            keep_second(f, s, dot(W1F[...], FI[s, pl.ds(f, 3)].reshape(3 * CH, width)))

    def back_second(f, s):
        p, q = f % 2, f // 2
        total = dot(W2B[...], CT[s, p, pl.ds(q, 3)].reshape(3 * CH, width))
        BS[s, f + 1] = (total * D2[s, f]).astype(BF16)

    for s in range(2, nr):
        second_inner(s)
    cot_near.start()
    first_middle.wait()
    for s in range(2, nr):
        second_outer(s)

    x_outer.wait()
    for f in outer:
        conv_row(place_of[f], f, 0, 0)
        conv_row(place_of[f], f, nr - 1, 1)
    first_edges.start()

    cot_far.wait()
    for s in range(2, nr):
        for f in outer:
            back_second(f, s)
    back_middle.start()

    x_inner.wait()
    for f in inner:
        conv_row(place_of[f], f, 0, 0)
        conv_row(place_of[f], f, nr - 1, 1)
    for s in range(2):
        second_inner(s)

    first_edges.wait()
    for s in range(2):
        second_outer(s)
        for f in outer:
            back_second(f, s)
    back_edges.start()

    cot_near.wait()
    for s in range(nr):
        for f in inner:
            back_second(f, s)

    def keep_back(f, h, value):
        at = place_of[f]
        value = value * D1[at, h]
        BF[at, h + 1] = value.astype(BF16)
        BFL[at, h] = from_right(value).astype(BF16)
        BFR[at, h] = from_left(value).astype(BF16)

    def back_inner(h, s):
        z = dot(W1B2[...], BS[s, pl.ds(1, 4)].reshape(4 * CH, width))
        keep_back(1, h, z[:CH])
        keep_back(2, h, z[CH:])

    def back_outer(h, s):
        for f in outer:
            keep_back(f, h, dot(W1B[...], BS[s, pl.ds(f, 3)].reshape(3 * CH, width)))

    back_inner(0, 0)
    back_inner(nr - 1, 1)
    rows_inner.start()
    for h in range(1, nr - 1):
        back_inner(h, h + 1)
    back_middle.wait()
    for h in range(1, nr - 1):
        back_outer(h, h + 1)

    low = lax.broadcasted_iota(jnp.int32, (CH, 2 * CH), 1) < CH

    def side_by_side(left, right):
        return jnp.where(low[: left.shape[0]], left, pltpu.roll(right, CH, 1))

    def reduce_scatter(pack, send, recv, which):
        rows = send.shape[1]
        for g in range(nxy):
            send[g] = pack[pl.ds(rows * g, rows), :]
        recv[me] = send[me]

        def one(d, _):
            g = lax.rem(me + d, nxy)
            copy_to(send.at[g], recv.at[me], which, xy_device(g)).start()
            return 0

        lax.fori_loop(1, nxy, one, 0)

    def copy_to(src, dst, which, device):
        return pltpu.make_async_remote_copy(
            src_ref=src, dst_ref=dst, send_sem=ars.at[which], recv_sem=arr.at[which],
            device_id=device, device_id_type=MESH,
        )

    def await_all(ref, count, sem):
        part = ref.at[pl.ds(0, count)]
        pltpu.make_async_copy(part, part, sem).wait()

    def added(ref):
        total = ref[0]
        for g in range(1, ref.shape[0]):
            total += ref[g]
        return total

    def exchange_tm(send, recv, spread, which):
        await_all(recv, nxy - 1, arr.at[which])
        await_all(send, nxy - 1, ars.at[which])
        spread[t] = added(recv)

        def one(d, _):
            s = lax.rem(t + d, ntm)
            copy_to(spread.at[t], spread.at[t], which + 1, tm_device(s)).start()
            return 0

        lax.fori_loop(1, ntm, one, 0)

    def gather_xy(spread, gathered, which):
        await_all(spread, ntm - 1, arr.at[which + 1])
        await_all(spread, ntm - 1, ars.at[which + 1])
        gathered[me] = added(spread)

        def one(d, _):
            g = lax.rem(me + d, nxy)
            copy_to(gathered.at[me], gathered.at[me], which + 2, xy_device(g)).start()
            return 0

        lax.fori_loop(1, nxy, one, 0)

    def unpack(packed, gathered, which):
        await_all(gathered, nxy - 1, arr.at[which + 2])
        await_all(gathered, nxy - 1, ars.at[which + 2])
        rows = gathered.shape[1]
        for g in range(nxy):
            packed[pl.ds(rows * g, rows), :] = gathered[g] * scale

    def lanes_of(parts):
        return jnp.concatenate(parts, axis=1)

    total1 = jnp.zeros((2 * CH, 4 * CH), F32)
    total2 = jnp.zeros((4 * CH, 2 * CH), F32)
    for s in range(0, nr, 2):
        at = [(s, 0), (s, 2), (s + 1, 0), (s + 1, 2)]
        total1 += dot_nt(
            lanes_of([BS[n, pl.ds(f + 1, 2)].reshape(2 * CH, width) for n, f in at]),
            lanes_of([FI[n, pl.ds(f, 4)].reshape(4 * CH, width) for n, f in at]),
        )
        at = [(s, 0), (s, 1), (s + 1, 0), (s + 1, 1)]
        total2 += dot_nt(
            lanes_of([CT[n, p].reshape(4 * CH, width) for n, p in at]),
            lanes_of([SE[n, p].reshape(2 * CH, width) for n, p in at]),
        )
    s1 = total1[:CH] + pltpu.roll(total1[CH:], 3 * CH, 1)
    s2 = total2[: 3 * CH] + pltpu.roll(total2[CH:], CH, 1)
    pack1[pl.ds(0, CH), :] = s1[:, : 2 * CH]
    pack1[pl.ds(CH, CH), :] = side_by_side(s1[:, 2 * CH :], s2[:CH])
    pack1[pl.ds(2 * CH, CH), :] = side_by_side(s2[CH : 2 * CH], s2[2 * CH :])
    reduce_scatter(pack1, a1s, a1r, 0)

    wide = [jnp.zeros((2 * CH, 4 * CH), F32)] * 3

    def versions(at, h, count):
        return (
            BFL[at, pl.ds(h, count)].reshape(count * CH, width),
            BF[at, pl.ds(h + 1, count)].reshape(count * CH, width),
            BFR[at, pl.ds(h, count)].reshape(count * CH, width),
        )

    def spatial(at_list, count):
        lefts = [versions(at, h, count) for at, h in at_list]
        right = lanes_of([X[at, pl.ds(h, count + 2)].reshape((count + 2) * CH, width) for at, h in at_list])
        left = jnp.concatenate([lanes_of([v[j] for v in lefts]) for j in range(3)], axis=0)
        return dot_nt(left, right)

    pairs = spatial([(0, h) for h in range(1, nr - 1, 2)], 2)
    for at in range(1, nf):
        pairs += spatial([(at, h) for h in range(1, nr - 1, 2)], 2)
    for j in range(3):
        total = pairs[2 * CH * j : 2 * CH * j + CH] + pltpu.roll(pairs[2 * CH * j + CH : 2 * CH * (j + 1)], 3 * CH, 1)
        wide[j] = total[:, : 3 * CH]

    back_edges.wait()
    back_outer(0, 0)
    back_outer(nr - 1, 1)
    singles = spatial([(at, h) for at in range(nf) for h in (0, nr - 1)], 1)
    tails = []
    for j in range(3):
        total = wide[j] + singles[CH * j : CH * (j + 1)]
        pack2[pl.ds(CH * j, CH), :] = total[:, : 2 * CH]
        tails.append(jnp.concatenate([total[:, 2 * CH :], total[:, 2 * CH :]], axis=1))
    pack2[pl.ds(3 * CH, CH), :] = jnp.where(low, tails[0], tails[1])
    pack2[pl.ds(4 * CH, half), :] = jnp.where(low[:half], tails[2][:half], tails[2][half:])
    reduce_scatter(pack2, a2s, a2r, 3)
    rows_outer.start()
    exchange_tm(a1s, a1r, b1r, 0)

    def grad_row(at, h):
        z = dot(WB[...], BF[at, pl.ds(h, 3)].reshape(3 * CH, width))
        value = z[CH : 2 * CH] + from_right(z[:CH]) + from_left(z[2 * CH :])
        IG[at, h] = value.astype(BF16)

    def hand_out(f):
        at = place_of[f]
        grad_row(at, 0)
        grad_row(at, nr - 1)
        for part in range(2):
            block = IG[at, :, pl.ds(half * part, half), :].reshape(half * nr, width)
            raw_o[pl.ds(half * part, half), f] = dot(POUT[...], block).reshape(half, nr, width).astype(BF16)

    def grad_inner(at, _):
        for h in range(1, nr - 1):
            grad_row(at, h)
        return 0

    lax.fori_loop(0, nf, grad_inner, 0)
    exchange_tm(a2s, a2r, b2r, 3)
    rows_inner.wait()
    for f in inner:
        hand_out(f)
    gather_xy(b1r, c1r, 0)
    rows_outer.wait()
    for f in outer:
        hand_out(f)
    gather_xy(b2r, c2r, 3)
    unpack(out1, c1r, 0)
    unpack(out2, c2r, 3)


def per_device(sizes, features, cotangent, w_spatial, w_first, w_second):
    _, ch, nf, nr, width = features.shape
    ntm, nheight, nbatch = sizes
    nxy = nheight * nbatch
    count = nbatch * nf * ntm * nr * nheight * width
    scale = 1.0 / math.sqrt(count)
    vmem = lambda shape, kind=BF16: pltpu.VMEM(shape, kind)
    all1, all2 = 3 * ch, 9 * ch // 2
    rows1, rows2 = all1 // nxy, all2 // nxy
    dma = pltpu.SemaphoreType.DMA
    scratch = [
        vmem((3, 3, ch, ch)), vmem((3, ch, ch)), vmem((3, ch, ch)),
        vmem((nf, ch, nr, width)), vmem((nf, ch, nr, width)),
        vmem((nf, nr + 2, ch, width)),
        vmem((nr, nf + 2, ch, width)),
        vmem((nf, nr, ch, width), F32),
        vmem((nr, nf, ch, width), F32),
        vmem((nr, 2, nf // 2 + 2, ch, width)),
        vmem((nr, 2, nf // 2, ch, width)),
        vmem((nr, nf + 2, ch, width)),
        vmem((nf, nr + 2, ch, width)),
        vmem((nf, nr, ch, width)), vmem((nf, nr, ch, width)), vmem((nf, nr, ch, width)),
        vmem((3 * ch, 3 * ch)), vmem((3 * ch, 3 * ch)),
        vmem((ch, 3 * ch)), vmem((ch, 3 * ch)), vmem((2 * ch, 4 * ch)), vmem((2 * ch, 4 * ch)), vmem((ch, 3 * ch)),
        vmem((ch // 2 * nr, ch // 2 * nr)), vmem((ch // 2 * nr, ch // 2 * nr)),
        vmem((all1, 2 * ch), F32), vmem((all2, 2 * ch), F32),
        vmem((nxy, rows1, 2 * ch), F32), vmem((nxy, rows1, 2 * ch), F32),
        vmem((ntm, rows1, 2 * ch), F32), vmem((nxy, rows1, 2 * ch), F32),
        vmem((nxy, rows2, 2 * ch), F32), vmem((nxy, rows2, 2 * ch), F32),
        vmem((ntm, rows2, 2 * ch), F32), vmem((nxy, rows2, 2 * ch), F32),
        dma((2 * nf + 3,)), dma((20,)), dma((20,)), dma((6,)), dma((6,)),
    ]
    here = pl.BlockSpec(memory_space=pltpu.VMEM)
    far = pl.BlockSpec(memory_space=pltpu.HBM)
    block, packed1, packed2 = pl.pallas_call(
        functools.partial(kernel, sizes, scale),
        out_shape=(
            jax.ShapeDtypeStruct((ch, nf, nr, width), BF16),
            jax.ShapeDtypeStruct((all1, 2 * ch), F32),
            jax.ShapeDtypeStruct((all2, 2 * ch), F32),
        ),
        in_specs=[far] * 5,
        out_specs=(here, here, here),
        scratch_shapes=scratch,
        compiler_params=pltpu.CompilerParams(
            collective_id=0, has_side_effects=True, vmem_limit_bytes=48 * 1024 * 1024
        ),
        name="critic_step",
    )(*(pltpu.with_memory_space_constraint(a, pltpu.HBM) for a in (features[0], cotangent[0], w_spatial, w_first, w_second)))
    input_grad, grad_spatial, grad_first, grad_second = pl.pallas_call(
        finish,
        out_shape=(
            jax.ShapeDtypeStruct((ch, nf, nr, width), BF16),
            jax.ShapeDtypeStruct((3, 3, ch, ch), F32),
            jax.ShapeDtypeStruct((3, ch, ch), F32),
            jax.ShapeDtypeStruct((3, ch, ch), F32),
        ),
        in_specs=[here] * 3,
        out_specs=(far, far, far, far),
        scratch_shapes=[
            vmem((3, 3, ch, ch), F32), vmem((3, ch, ch), F32), vmem((3, ch, ch), F32), dma((4,)),
        ],
        compiler_params=pltpu.CompilerParams(vmem_limit_bytes=8 * 1024 * 1024),
        name="hand_out_results",
    )(packed1, packed2, block)
    return input_grad[None], grad_spatial, grad_first, grad_second


def solution(mesh):
    sizes = tuple(mesh.shape[axis] for axis in AXES)
    big = P("batch", None, "tm", "height", None)
    return jax.shard_map(
        functools.partial(per_device, sizes),
        mesh=mesh,
        in_specs=(big, big, P(), P(), P()),
        out_specs=(big, P(), P(), P()),
        check_vma=False,
    )
```

```python
import functools
import math

import jax
import jax.numpy as jnp
from jax import lax
from jax.experimental import pallas as pl
from jax.experimental.pallas import tpu as pltpu
from jax.sharding import PartitionSpec as P

BF16 = jnp.bfloat16
F32 = jnp.float32
MESH = pl.DeviceIdType.MESH
CH = 64
AXES = ("tm", "height", "batch")


def dot(left, right):
    return jnp.dot(left, right, preferred_element_type=F32)


def dot_nt(left, right):
    return lax.dot_general(left, right, (((1,), (1,)), ((), ())), preferred_element_type=F32)


def gate(value):
    t = jnp.tanh(0.5 * value)
    g = 0.6 + 0.4 * t
    return value * g, g + 0.2 * value * (1.0 - t * t)


def finish(packed1, packed2, block, out, gs, g1, g2, gs_v, g1_v, g2_v, sems):
    big = pltpu.make_async_copy(block, out, sems.at[0])
    big.start()
    half = CH // 2
    g1_v[0] = packed1[pl.ds(0, CH), :CH]
    g1_v[1] = packed1[pl.ds(0, CH), CH:]
    g1_v[2] = packed1[pl.ds(CH, CH), :CH]
    g2_v[2] = packed1[pl.ds(CH, CH), CH:]
    g2_v[1] = packed1[pl.ds(2 * CH, CH), :CH]
    g2_v[0] = packed1[pl.ds(2 * CH, CH), CH:]
    for j in range(3):
        gs_v[0, j] = packed2[pl.ds(CH * j, CH), :CH]
        gs_v[1, j] = packed2[pl.ds(CH * j, CH), CH:]
    gs_v[2, 0] = packed2[pl.ds(3 * CH, CH), :CH]
    gs_v[2, 1] = packed2[pl.ds(3 * CH, CH), CH:]
    gs_v[2, 2, pl.ds(0, half), :] = packed2[pl.ds(4 * CH, half), :CH]
    gs_v[2, 2, pl.ds(half, half), :] = packed2[pl.ds(4 * CH, half), CH:]
    small = [
        pltpu.make_async_copy(source, target, sems.at[1 + n])
        for n, (source, target) in enumerate(((gs_v, gs), (g1_v, g1), (g2_v, g2)))
    ]
    for copy in small:
        copy.start()
    for copy in small:
        copy.wait()
    big.wait()


def kernel(
    sizes, scale,
    feat, cot, ws_hbm, w1_hbm, w2_hbm,
    raw_o, out1, out2,
    ws, w1, w2, raw_f, raw_c, X, FI, D1, D2, CT, SE, BS, BF, BFL, BFR, IG,
    WF, WB, W1F, W1B, W1F2, W1B2, W2B, PIN, POUT,
    pack1, pack2,
    a1s, a1r, b1r, c1r, a2s, a2r, b2r, c2r,
    sem_in, sends, recvs, ars, arr, known,
):
    ntm, nheight, nbatch = sizes
    nxy = nheight * nbatch
    nf, nr, width = raw_f.shape[0], raw_f.shape[2], raw_f.shape[3]
    last = nf - 1
    place_of = {0: 0, last: 1, 1: 2, 2: 3}
    outer, inner = (0, last), (1, 2)
    t = lax.axis_index("tm")
    hh = lax.axis_index("height")
    b = lax.axis_index("batch")
    me = hh * nbatch + b
    before = (lax.rem(t + ntm - 1, ntm), hh, b)
    after = (lax.rem(t + 1, ntm), hh, b)
    above = (t, hh - 1, b)
    below = (t, hh + 1, b)
    has_above = hh > 0
    has_below = hh < nheight - 1

    def xy_device(g):
        return (t, g // nbatch, lax.rem(g, nbatch))

    def tm_device(s):
        return (s, hh, b)

    barrier = pltpu.get_barrier_semaphore()

    beside = (t, hh, nbatch - 1 - b)

    def tell(sem, distance, along_tm):
        if along_tm:
            for d in (distance, ntm - distance):
                pl.semaphore_signal(sem, inc=1, device_id=(lax.rem(t + d, ntm), hh, b), device_id_type=MESH)

        @pl.when(hh >= distance)
        def _():
            pl.semaphore_signal(sem, inc=1, device_id=(t, hh - distance, b), device_id_type=MESH)

        @pl.when(hh + distance < nheight)
        def _():
            pl.semaphore_signal(sem, inc=1, device_id=(t, hh + distance, b), device_id_type=MESH)

    def hear(sem, distance, along_tm, others=0):
        upper = (hh + nheight - distance) // nheight
        lower = (2 * nheight - 1 - distance - hh) // nheight
        pl.semaphore_wait(sem, upper + lower + 2 * along_tm + others)

    rounds = [(n, d, d < ntm // 2) for n, d in enumerate((1, 2, 4)) if d < nheight or d < ntm // 2]

    def pass_on(n):
        if n > 0 and n <= len(rounds):
            _, d, along_tm = rounds[n - 1]
            hear(known.at[n - 1], d, along_tm)
        if n < len(rounds):
            _, d, along_tm = rounds[n]
            tell(known.at[n], d, along_tm)
        if n == 3 and nbatch == 2:
            pl.semaphore_signal(known.at[3], inc=1, device_id=beside, device_id_type=MESH)
        if n == 4 and nbatch == 2:
            pl.semaphore_wait(known.at[3], 1)

    loads_w = [
        pltpu.make_async_copy(source, target, sem_in.at[2 * nf + n])
        for n, (source, target) in enumerate(((ws_hbm, ws), (w1_hbm, w1), (w2_hbm, w2)))
    ]
    loads_f = [pltpu.make_async_copy(feat.at[:, f], raw_f.at[f], sem_in.at[f]) for f in range(nf)]
    loads_c = [pltpu.make_async_copy(cot.at[:, f], raw_c.at[f + 2], sem_in.at[nf + f]) for f in range(nf)]
    for copy in loads_w + loads_f:
        copy.start()
    tell(barrier, 1, True)
    if nbatch == 2:
        pl.semaphore_signal(barrier, inc=1, device_id=beside, device_id_type=MESH)
    for copy in loads_c:
        copy.start()

    row = lax.broadcasted_iota(jnp.int32, (CH, 4 * CH), 0)
    col = lax.broadcasted_iota(jnp.int32, (CH, 4 * CH), 1)
    place = [jnp.where(col == row + CH * i, 1.0, 0.0).astype(BF16) for i in range(4)]
    eye = place[0][:, :CH]
    half = CH // 2
    prow = lax.broadcasted_iota(jnp.int32, (half * nr, half * nr), 0)
    pcol = lax.broadcasted_iota(jnp.int32, (half * nr, half * nr), 1)
    PIN[...] = jnp.where(pcol == lax.rem(prow, half) * nr + prow // half, 1.0, 0.0).astype(BF16)
    POUT[...] = jnp.where(prow == lax.rem(pcol, half) * nr + pcol // half, 1.0, 0.0).astype(BF16)
    edge = jnp.zeros((nf, CH, width), BF16)

    @pl.when(jnp.logical_not(has_above))
    def _():
        X[:, 0] = edge
        BF[:, 0] = edge

    @pl.when(jnp.logical_not(has_below))
    def _():
        X[:, nr + 1] = edge
        BF[:, nr + 1] = edge

    def side(parts, at):
        total = dot(parts[0], place[at])
        for i in range(1, len(parts)):
            total += dot(parts[i], place[at + i])
        return total.astype(BF16)

    def turned(parts):
        return dot_nt(eye, jnp.concatenate(parts, axis=0)).astype(BF16)

    for copy in loads_w:
        copy.wait()
    for j in range(3):
        WF[pl.ds(CH * j, CH), :] = side([ws[0, j], ws[1, j], ws[2, j]], 0)[:, : 3 * CH]
        WB[pl.ds(CH * j, CH), :] = turned([ws[2, j], ws[1, j], ws[0, j]])
    none = jnp.zeros((CH, CH), BF16)
    W1F[...] = side([w1[0], w1[1], w1[2]], 0)[:, : 3 * CH]
    W1B[...] = turned([w1[2], w1[1], w1[0]])
    W2B[...] = turned([w2[2], w2[1], w2[0]])
    for a in range(2):
        W1F2[pl.ds(CH * a, CH), :] = side([w1[0], w1[1], w1[2]], a)
        W1B2[pl.ds(CH * a, CH), :] = turned([none] * a + [w1[2], w1[1], w1[0]] + [none] * (1 - a))

    lane = lax.broadcasted_iota(jnp.int32, (CH, width), 1)

    def from_left(value):
        return jnp.where(lane == 0, 0.0, pltpu.roll(value, 1, 1))

    def from_right(value):
        return jnp.where(lane == width - 1, 0.0, pltpu.roll(value, width - 1, 1))

    def to_rows(raw, part):
        block = raw[pl.ds(half * part, half)].astype(F32).reshape(half * nr, width).astype(BF16)
        return dot(PIN[...], block).astype(BF16).reshape(nr, half, width)

    def conv_row(at, f, h, s):
        z = dot(WF[...], X[at, pl.ds(h, 3)].reshape(3 * CH, width))
        value = z[CH : 2 * CH] + from_left(z[:CH]) + from_right(z[2 * CH :])
        act, der = gate(value)
        FI[s, f + 1] = act.astype(BF16)
        D1[at, h] = der

    def cot_rows(k):
        for part in range(2):
            lanes = pl.ds(half * part, half)
            block = to_rows(raw_c.at[k], part)
            CT[0, k % 2, k // 2, lanes, :] = block[0]
            CT[1, k % 2, k // 2, lanes, :] = block[nr - 1]
            CT[pl.ds(2, nr - 2), k % 2, k // 2, lanes, :] = block[1 : nr - 1]

    for f in outer + inner:
        loads_f[f].wait()
        for part in range(2):
            X[place_of[f], pl.ds(1, nr), pl.ds(half * part, half), :] = to_rows(raw_f.at[f], part)
    for f in outer:
        for h in range(1, nr - 1):
            conv_row(place_of[f], f, h, h + 1)

    hear(barrier, 1, True, nbatch - 1)

    used = [0]

    def remote(src, dst, device):
        n = used[0]
        used[0] += 1
        return pltpu.make_async_remote_copy(
            src_ref=src, dst_ref=dst, send_sem=sends.at[n], recv_sem=recvs.at[n],
            device_id=device, device_id_type=MESH,
        )

    class Rows:
        def __init__(self, array, frames):
            self.up = remote(array.at[frames, 1], array.at[frames, nr + 1], above)
            self.down = remote(array.at[frames, nr], array.at[frames, 0], below)

        def start(self):
            pl.when(has_above)(self.up.start)
            pl.when(has_below)(self.down.start)

        def wait(self):
            pl.when(has_above)(self.down.wait_recv)
            pl.when(has_below)(self.up.wait_recv)

        def drain(self):
            pl.when(has_above)(self.up.wait_send)
            pl.when(has_below)(self.down.wait_send)

    class Frames:
        def __init__(self, back_src, back_dst, fore_src, fore_dst):
            self.both = (remote(back_src, back_dst, before), remote(fore_src, fore_dst, after))

        def start(self):
            for copy in self.both:
                copy.start()

        def wait(self):
            for copy in self.both:
                copy.wait_recv()

        def drain(self):
            for copy in self.both:
                copy.wait_send()

    def outer_frames(array, rows):
        return Frames(array.at[rows, 1], array.at[rows, nf + 1], array.at[rows, nf], array.at[rows, 0])

    edges, middle = pl.ds(0, 2), pl.ds(2, nr - 2)
    first_two, second_two = pl.ds(0, 2), pl.ds(2, 2)
    x_outer, x_inner = Rows(X, first_two), Rows(X, second_two)
    first_middle, first_edges = outer_frames(FI, middle), outer_frames(FI, edges)
    cot_far = Frames(cot.at[:, 1], raw_c.at[nf + 3], cot.at[:, nf - 2], raw_c.at[0])
    cot_near = Frames(cot.at[:, 0], raw_c.at[nf + 2], cot.at[:, nf - 1], raw_c.at[1])
    back_middle, back_edges = outer_frames(BS, middle), outer_frames(BS, edges)
    rows_inner, rows_outer = Rows(BF, second_two), Rows(BF, first_two)

    x_outer.start()
    first_middle.start()
    cot_far.start()
    pass_on(0)
    for f in inner:
        for h in range(1, nr - 1):
            conv_row(place_of[f], f, h, h + 1)

    def keep_second(f, s, value):
        act, der = gate(value)
        SE[s, f % 2, f // 2] = act.astype(BF16)
        D2[s, f] = der

    def second_inner(s):
        z = dot(W1F2[...], FI[s, pl.ds(1, 4)].reshape(4 * CH, width))
        keep_second(1, s, z[:CH])
        keep_second(2, s, z[CH:])

    def second_outer(s):
        for f in outer:
            keep_second(f, s, dot(W1F[...], FI[s, pl.ds(f, 3)].reshape(3 * CH, width)))

    def back_second(f, s):
        p, q = f % 2, f // 2
        total = dot(W2B[...], CT[s, p, pl.ds(q, 3)].reshape(3 * CH, width))
        BS[s, f + 1] = (total * D2[s, f]).astype(BF16)

    for s in range(2, nr):
        second_inner(s)
    for f in range(nf):
        loads_c[f].wait()
        cot_rows(f + 2)
    x_inner.start()
    cot_near.start()
    pass_on(1)
    first_middle.wait()
    for s in range(2, nr):
        second_outer(s)

    x_outer.wait()
    for f in outer:
        conv_row(place_of[f], f, 0, 0)
        conv_row(place_of[f], f, nr - 1, 1)
    first_edges.start()

    cot_far.wait()
    cot_rows(0)
    cot_rows(nf + 3)
    for s in range(2, nr):
        for f in outer:
            back_second(f, s)
    back_middle.start()

    pass_on(2)
    x_inner.wait()
    for f in inner:
        conv_row(place_of[f], f, 0, 0)
        conv_row(place_of[f], f, nr - 1, 1)
    for s in range(2):
        second_inner(s)

    first_edges.wait()
    for s in range(2):
        second_outer(s)
        for f in outer:
            back_second(f, s)
    back_edges.start()

    pass_on(3)
    cot_near.wait()
    cot_rows(1)
    cot_rows(nf + 2)
    for s in range(nr):
        for f in inner:
            back_second(f, s)

    def keep_back(f, h, value):
        at = place_of[f]
        value = value * D1[at, h]
        BF[at, h + 1] = value.astype(BF16)
        BFL[at, h] = from_right(value).astype(BF16)
        BFR[at, h] = from_left(value).astype(BF16)

    def back_inner(h, s):
        z = dot(W1B2[...], BS[s, pl.ds(1, 4)].reshape(4 * CH, width))
        keep_back(1, h, z[:CH])
        keep_back(2, h, z[CH:])

    def back_outer(h, s):
        for f in outer:
            keep_back(f, h, dot(W1B[...], BS[s, pl.ds(f, 3)].reshape(3 * CH, width)))

    back_inner(0, 0)
    back_inner(nr - 1, 1)
    rows_inner.start()
    for h in range(1, nr - 1):
        back_inner(h, h + 1)
    back_middle.wait()
    for h in range(1, nr - 1):
        back_outer(h, h + 1)

    low = lax.broadcasted_iota(jnp.int32, (CH, 2 * CH), 1) < CH

    def side_by_side(left, right):
        return jnp.where(low[: left.shape[0]], left, pltpu.roll(right, CH, 1))

    def reduce_scatter(pack, send, recv, which):
        rows = send.shape[1]
        for g in range(nxy):
            send[g] = pack[pl.ds(rows * g, rows), :]
        recv[me] = send[me]

        def one(d, _):
            g = lax.rem(me + d, nxy)
            copy_to(send.at[g], recv.at[me], which, xy_device(g)).start()
            return 0

        lax.fori_loop(1, nxy, one, 0)

    def copy_to(src, dst, which, device):
        return pltpu.make_async_remote_copy(
            src_ref=src, dst_ref=dst, send_sem=ars.at[which], recv_sem=arr.at[which],
            device_id=device, device_id_type=MESH,
        )

    def await_all(ref, count, sem):
        part = ref.at[pl.ds(0, count)]
        pltpu.make_async_copy(part, part, sem).wait()

    def added(ref):
        total = ref[0]
        for g in range(1, ref.shape[0]):
            total += ref[g]
        return total

    def exchange_tm(send, recv, spread, which):
        await_all(recv, nxy - 1, arr.at[which])
        spread[t] = added(recv)

        def one(d, _):
            s = lax.rem(t + d, ntm)
            copy_to(spread.at[t], spread.at[t], which + 1, tm_device(s)).start()
            return 0

        lax.fori_loop(1, ntm, one, 0)

    def gather_xy(spread, gathered, which):
        await_all(spread, ntm - 1, arr.at[which + 1])
        gathered[me] = added(spread)

        def one(d, _):
            g = lax.rem(me + d, nxy)
            copy_to(gathered.at[me], gathered.at[me], which + 2, xy_device(g)).start()
            return 0

        lax.fori_loop(1, nxy, one, 0)

    def unpack(packed, gathered, which):
        await_all(gathered, nxy - 1, arr.at[which + 2])
        rows = gathered.shape[1]
        for g in range(nxy):
            packed[pl.ds(rows * g, rows), :] = gathered[g] * scale

    def lanes_of(parts):
        return jnp.concatenate(parts, axis=1)

    total1 = jnp.zeros((2 * CH, 4 * CH), F32)
    total2 = jnp.zeros((4 * CH, 2 * CH), F32)
    for s in range(0, nr, 2):
        at = [(s, 0), (s, 2), (s + 1, 0), (s + 1, 2)]
        total1 += dot_nt(
            lanes_of([BS[n, pl.ds(f + 1, 2)].reshape(2 * CH, width) for n, f in at]),
            lanes_of([FI[n, pl.ds(f, 4)].reshape(4 * CH, width) for n, f in at]),
        )
        at = [(s, 0), (s, 1), (s + 1, 0), (s + 1, 1)]
        total2 += dot_nt(
            lanes_of([CT[n, p].reshape(4 * CH, width) for n, p in at]),
            lanes_of([SE[n, p].reshape(2 * CH, width) for n, p in at]),
        )
    s1 = total1[:CH] + pltpu.roll(total1[CH:], 3 * CH, 1)
    s2 = total2[: 3 * CH] + pltpu.roll(total2[CH:], CH, 1)
    pack1[pl.ds(0, CH), :] = s1[:, : 2 * CH]
    pack1[pl.ds(CH, CH), :] = side_by_side(s1[:, 2 * CH :], s2[:CH])
    pack1[pl.ds(2 * CH, CH), :] = side_by_side(s2[CH : 2 * CH], s2[2 * CH :])
    pass_on(4)
    reduce_scatter(pack1, a1s, a1r, 0)

    wide = [jnp.zeros((2 * CH, 4 * CH), F32)] * 3

    def versions(at, h, count):
        return (
            BFL[at, pl.ds(h, count)].reshape(count * CH, width),
            BF[at, pl.ds(h + 1, count)].reshape(count * CH, width),
            BFR[at, pl.ds(h, count)].reshape(count * CH, width),
        )

    def spatial(at_list, count):
        lefts = [versions(at, h, count) for at, h in at_list]
        right = lanes_of([X[at, pl.ds(h, count + 2)].reshape((count + 2) * CH, width) for at, h in at_list])
        left = jnp.concatenate([lanes_of([v[j] for v in lefts]) for j in range(3)], axis=0)
        return dot_nt(left, right)

    pairs = spatial([(0, h) for h in range(1, nr - 1, 2)], 2)
    for at in range(1, nf):
        pairs += spatial([(at, h) for h in range(1, nr - 1, 2)], 2)
    for j in range(3):
        total = pairs[2 * CH * j : 2 * CH * j + CH] + pltpu.roll(pairs[2 * CH * j + CH : 2 * CH * (j + 1)], 3 * CH, 1)
        wide[j] = total[:, : 3 * CH]

    back_edges.wait()
    back_outer(0, 0)
    back_outer(nr - 1, 1)
    singles = spatial([(at, h) for at in range(nf) for h in (0, nr - 1)], 1)
    tails = []
    for j in range(3):
        total = wide[j] + singles[CH * j : CH * (j + 1)]
        pack2[pl.ds(CH * j, CH), :] = total[:, : 2 * CH]
        tails.append(jnp.concatenate([total[:, 2 * CH :], total[:, 2 * CH :]], axis=1))
    pack2[pl.ds(3 * CH, CH), :] = jnp.where(low, tails[0], tails[1])
    pack2[pl.ds(4 * CH, half), :] = jnp.where(low[:half], tails[2][:half], tails[2][half:])
    reduce_scatter(pack2, a2s, a2r, 3)
    exchange_tm(a1s, a1r, b1r, 0)

    def grad_row(at, h):
        z = dot(WB[...], BF[at, pl.ds(h, 3)].reshape(3 * CH, width))
        value = z[CH : 2 * CH] + from_right(z[:CH]) + from_left(z[2 * CH :])
        IG[at, h] = value.astype(BF16)

    def hand_out(f):
        at = place_of[f]
        grad_row(at, 0)
        grad_row(at, nr - 1)
        for part in range(2):
            block = IG[at, :, pl.ds(half * part, half), :].reshape(half * nr, width)
            raw_o[pl.ds(half * part, half), f] = dot(POUT[...], block).reshape(half, nr, width).astype(BF16)

    def grad_inner(at, _):
        for h in range(1, nr - 1):
            grad_row(at, h)
        return 0

    lax.fori_loop(0, nf, grad_inner, 0)
    exchange_tm(a2s, a2r, b2r, 3)
    rows_outer.start()
    rows_inner.wait()
    for f in inner:
        hand_out(f)
    gather_xy(b1r, c1r, 0)
    rows_outer.wait()
    for f in outer:
        hand_out(f)
    gather_xy(b2r, c2r, 3)
    unpack(out1, c1r, 0)
    unpack(out2, c2r, 3)
    halos = (x_outer, x_inner, first_middle, first_edges, cot_far, cot_near)
    for halo in halos + (back_middle, back_edges, rows_inner, rows_outer):
        halo.drain()
    for which, sent in ((0, (a1s, b1r, c1r)), (3, (a2s, b2r, c2r))):
        for n, count in enumerate((nxy, ntm, nxy)):
            await_all(sent[n], count - 1, ars.at[which + n])


def per_device(sizes, features, cotangent, w_spatial, w_first, w_second):
    _, ch, nf, nr, width = features.shape
    ntm, nheight, nbatch = sizes
    nxy = nheight * nbatch
    count = nbatch * nf * ntm * nr * nheight * width
    scale = 1.0 / math.sqrt(count)
    vmem = lambda shape, kind=BF16: pltpu.VMEM(shape, kind)
    all1, all2 = 3 * ch, 9 * ch // 2
    rows1, rows2 = all1 // nxy, all2 // nxy
    dma = pltpu.SemaphoreType.DMA
    scratch = [
        vmem((3, 3, ch, ch)), vmem((3, ch, ch)), vmem((3, ch, ch)),
        vmem((nf, ch, nr, width)), vmem((nf + 4, ch, nr, width)),
        vmem((nf, nr + 2, ch, width)),
        vmem((nr, nf + 2, ch, width)),
        vmem((nf, nr, ch, width), F32),
        vmem((nr, nf, ch, width), F32),
        vmem((nr, 2, nf // 2 + 2, ch, width)),
        vmem((nr, 2, nf // 2, ch, width)),
        vmem((nr, nf + 2, ch, width)),
        vmem((nf, nr + 2, ch, width)),
        vmem((nf, nr, ch, width)), vmem((nf, nr, ch, width)), vmem((nf, nr, ch, width)),
        vmem((3 * ch, 3 * ch)), vmem((3 * ch, 3 * ch)),
        vmem((ch, 3 * ch)), vmem((ch, 3 * ch)), vmem((2 * ch, 4 * ch)), vmem((2 * ch, 4 * ch)), vmem((ch, 3 * ch)),
        vmem((ch // 2 * nr, ch // 2 * nr)), vmem((ch // 2 * nr, ch // 2 * nr)),
        vmem((all1, 2 * ch), F32), vmem((all2, 2 * ch), F32),
        vmem((nxy, rows1, 2 * ch), F32), vmem((nxy, rows1, 2 * ch), F32),
        vmem((ntm, rows1, 2 * ch), F32), vmem((nxy, rows1, 2 * ch), F32),
        vmem((nxy, rows2, 2 * ch), F32), vmem((nxy, rows2, 2 * ch), F32),
        vmem((ntm, rows2, 2 * ch), F32), vmem((nxy, rows2, 2 * ch), F32),
        dma((2 * nf + 3,)), dma((20,)), dma((20,)), dma((6,)), dma((6,)), pltpu.SemaphoreType.REGULAR((4,)),
    ]
    here = pl.BlockSpec(memory_space=pltpu.VMEM)
    far = pl.BlockSpec(memory_space=pltpu.HBM)
    block, packed1, packed2 = pl.pallas_call(
        functools.partial(kernel, sizes, scale),
        out_shape=(
            jax.ShapeDtypeStruct((ch, nf, nr, width), BF16),
            jax.ShapeDtypeStruct((all1, 2 * ch), F32),
            jax.ShapeDtypeStruct((all2, 2 * ch), F32),
        ),
        in_specs=[far] * 5,
        out_specs=(here, here, here),
        scratch_shapes=scratch,
        compiler_params=pltpu.CompilerParams(
            collective_id=0, has_side_effects=True, vmem_limit_bytes=48 * 1024 * 1024
        ),
        name="critic_step",
    )(*(pltpu.with_memory_space_constraint(a, pltpu.HBM) for a in (features[0], cotangent[0], w_spatial, w_first, w_second)))
    input_grad, grad_spatial, grad_first, grad_second = pl.pallas_call(
        finish,
        out_shape=(
            jax.ShapeDtypeStruct((ch, nf, nr, width), BF16),
            jax.ShapeDtypeStruct((3, 3, ch, ch), F32),
            jax.ShapeDtypeStruct((3, ch, ch), F32),
            jax.ShapeDtypeStruct((3, ch, ch), F32),
        ),
        in_specs=[here] * 3,
        out_specs=(far, far, far, far),
        scratch_shapes=[
            vmem((3, 3, ch, ch), F32), vmem((3, ch, ch), F32), vmem((3, ch, ch), F32), dma((4,)),
        ],
        compiler_params=pltpu.CompilerParams(vmem_limit_bytes=8 * 1024 * 1024),
        name="hand_out_results",
    )(packed1, packed2, block)
    return input_grad[None], grad_spatial, grad_first, grad_second


def solution(mesh):
    sizes = tuple(mesh.shape[axis] for axis in AXES)
    big = P("batch", None, "tm", "height", None)
    return jax.shard_map(
        functools.partial(per_device, sizes),
        mesh=mesh,
        in_specs=(big, big, P(), P(), P()),
        out_specs=(big, P(), P(), P()),
        check_vma=False,
    )
```

```python
import functools
import math

import jax
import jax.numpy as jnp
from jax import lax
from jax.experimental import pallas as pl
from jax.experimental.pallas import tpu as pltpu
from jax.sharding import PartitionSpec as P

BF16 = jnp.bfloat16
F32 = jnp.float32
MESH = pl.DeviceIdType.MESH
CH = 64
AXES = ("tm", "height", "batch")


def dot(left, right):
    return jnp.dot(left, right, preferred_element_type=F32)


def dot_nt(left, right):
    return lax.dot_general(left, right, (((1,), (1,)), ((), ())), preferred_element_type=F32)


def gate(value):
    t = jnp.tanh(0.5 * value)
    g = 0.6 + 0.4 * t
    return value * g, g + 0.2 * value * (1.0 - t * t)


def finish(packed1, packed2, block, out, gs, g1, g2, gs_v, g1_v, g2_v, sems):
    big = pltpu.make_async_copy(block, out, sems.at[0])
    big.start()
    half = CH // 2
    g1_v[0] = packed1[pl.ds(0, CH), :CH]
    g1_v[1] = packed1[pl.ds(0, CH), CH:]
    g1_v[2] = packed1[pl.ds(CH, CH), :CH]
    g2_v[2] = packed1[pl.ds(CH, CH), CH:]
    g2_v[1] = packed1[pl.ds(2 * CH, CH), :CH]
    g2_v[0] = packed1[pl.ds(2 * CH, CH), CH:]
    for j in range(3):
        gs_v[0, j] = packed2[pl.ds(CH * j, CH), :CH]
        gs_v[1, j] = packed2[pl.ds(CH * j, CH), CH:]
    gs_v[2, 0] = packed2[pl.ds(3 * CH, CH), :CH]
    gs_v[2, 1] = packed2[pl.ds(3 * CH, CH), CH:]
    gs_v[2, 2, pl.ds(0, half), :] = packed2[pl.ds(4 * CH, half), :CH]
    gs_v[2, 2, pl.ds(half, half), :] = packed2[pl.ds(4 * CH, half), CH:]
    small = [
        pltpu.make_async_copy(source, target, sems.at[1 + n])
        for n, (source, target) in enumerate(((gs_v, gs), (g1_v, g1), (g2_v, g2)))
    ]
    for copy in small:
        copy.start()
    for copy in small:
        copy.wait()
    big.wait()


def kernel(
    sizes, scale,
    feat, cot, ws_hbm, w1_hbm, w2_hbm,
    raw_o, out1, out2,
    ws, w1, w2, raw_f, raw_c, X, FI, D1, D2, CT, SE, BS, BF, BFL, BFR, IG,
    WF, WB, W1F, W1B, W1F2, W1B2, W2B, PIN, POUT,
    pack1, pack2,
    a1s, a1r, b1r, c1r, a2s, a2r, b2r, c2r,
    sem_in, sends, recvs, ars, arr, known,
):
    ntm, nheight, nbatch = sizes
    nxy = nheight * nbatch
    nf, nr, width = raw_f.shape[0], raw_f.shape[2], raw_f.shape[3]
    last = nf - 1
    place_of = {0: 0, last: 1, 1: 2, 2: 3}
    outer, inner = (0, last), (1, 2)
    t = lax.axis_index("tm")
    hh = lax.axis_index("height")
    b = lax.axis_index("batch")
    me = hh * nbatch + b
    before = (lax.rem(t + ntm - 1, ntm), hh, b)
    after = (lax.rem(t + 1, ntm), hh, b)
    above = (t, hh - 1, b)
    below = (t, hh + 1, b)
    has_above = hh > 0
    has_below = hh < nheight - 1

    def xy_device(g):
        return (t, g // nbatch, lax.rem(g, nbatch))

    def tm_device(s):
        return (s, hh, b)

    barrier = pltpu.get_barrier_semaphore()

    beside = (t, hh, nbatch - 1 - b)

    def tell(sem, distance, along_tm):
        if along_tm:
            for d in (distance, ntm - distance):
                pl.semaphore_signal(sem, inc=1, device_id=(lax.rem(t + d, ntm), hh, b), device_id_type=MESH)

        @pl.when(hh >= distance)
        def _():
            pl.semaphore_signal(sem, inc=1, device_id=(t, hh - distance, b), device_id_type=MESH)

        @pl.when(hh + distance < nheight)
        def _():
            pl.semaphore_signal(sem, inc=1, device_id=(t, hh + distance, b), device_id_type=MESH)

    def hear(sem, distance, along_tm, others=0):
        upper = (hh + nheight - distance) // nheight
        lower = (2 * nheight - 1 - distance - hh) // nheight
        pl.semaphore_wait(sem, upper + lower + 2 * along_tm + others)

    rounds = [(n, d, d < ntm // 2) for n, d in enumerate((1, 2, 4)) if d < nheight or d < ntm // 2]

    def pass_on(n):
        if n > 0 and n <= len(rounds):
            _, d, along_tm = rounds[n - 1]
            hear(known.at[n - 1], d, along_tm)
        if n < len(rounds):
            _, d, along_tm = rounds[n]
            tell(known.at[n], d, along_tm)
        if n == 3 and nbatch == 2:
            pl.semaphore_signal(known.at[3], inc=1, device_id=beside, device_id_type=MESH)
        if n == 4 and nbatch == 2:
            pl.semaphore_wait(known.at[3], 1)

    loads_w = [
        pltpu.make_async_copy(source, target, sem_in.at[2 * nf + n])
        for n, (source, target) in enumerate(((ws_hbm, ws), (w1_hbm, w1), (w2_hbm, w2)))
    ]
    loads_f = [pltpu.make_async_copy(feat.at[:, f], raw_f.at[f], sem_in.at[f]) for f in range(nf)]
    loads_c = [pltpu.make_async_copy(cot.at[:, f], raw_c.at[f + 2], sem_in.at[nf + f]) for f in range(nf)]
    for copy in loads_w + loads_f:
        copy.start()
    tell(barrier, 1, True)
    if nbatch == 2:
        pl.semaphore_signal(barrier, inc=1, device_id=beside, device_id_type=MESH)
    for copy in loads_c:
        copy.start()

    row = lax.broadcasted_iota(jnp.int32, (CH, 4 * CH), 0)
    col = lax.broadcasted_iota(jnp.int32, (CH, 4 * CH), 1)
    place = [jnp.where(col == row + CH * i, 1.0, 0.0).astype(BF16) for i in range(4)]
    eye = place[0][:, :CH]
    half = CH // 2
    prow = lax.broadcasted_iota(jnp.int32, (half * nr, half * nr), 0)
    pcol = lax.broadcasted_iota(jnp.int32, (half * nr, half * nr), 1)
    PIN[...] = jnp.where(pcol == lax.rem(prow, half) * nr + prow // half, 1.0, 0.0).astype(BF16)
    POUT[...] = jnp.where(prow == lax.rem(pcol, half) * nr + pcol // half, 1.0, 0.0).astype(BF16)
    edge = jnp.zeros((nf, CH, width), BF16)

    @pl.when(jnp.logical_not(has_above))
    def _():
        X[:, 0] = edge
        BF[:, 0] = edge

    @pl.when(jnp.logical_not(has_below))
    def _():
        X[:, nr + 1] = edge
        BF[:, nr + 1] = edge

    def side(parts, at):
        total = dot(parts[0], place[at])
        for i in range(1, len(parts)):
            total += dot(parts[i], place[at + i])
        return total.astype(BF16)

    def turned(parts):
        return dot_nt(eye, jnp.concatenate(parts, axis=0)).astype(BF16)

    for copy in loads_w:
        copy.wait()
    for j in range(3):
        WF[pl.ds(CH * j, CH), :] = side([ws[0, j], ws[1, j], ws[2, j]], 0)[:, : 3 * CH]
        WB[pl.ds(CH * j, CH), :] = turned([ws[2, j], ws[1, j], ws[0, j]])
    none = jnp.zeros((CH, CH), BF16)
    W1F[...] = side([w1[0], w1[1], w1[2]], 0)[:, : 3 * CH]
    W1B[...] = turned([w1[2], w1[1], w1[0]])
    W2B[...] = turned([w2[2], w2[1], w2[0]])
    for a in range(2):
        W1F2[pl.ds(CH * a, CH), :] = side([w1[0], w1[1], w1[2]], a)
        W1B2[pl.ds(CH * a, CH), :] = turned([none] * a + [w1[2], w1[1], w1[0]] + [none] * (1 - a))

    lane = lax.broadcasted_iota(jnp.int32, (CH, width), 1)

    def from_left(value):
        return jnp.where(lane == 0, 0.0, pltpu.roll(value, 1, 1))

    def from_right(value):
        return jnp.where(lane == width - 1, 0.0, pltpu.roll(value, width - 1, 1))

    def to_rows(raw, part):
        block = raw[pl.ds(half * part, half)].astype(F32).reshape(half * nr, width).astype(BF16)
        return dot(PIN[...], block).astype(BF16).reshape(nr, half, width)

    def conv_row(at, f, h, s):
        z = dot(WF[...], X[at, pl.ds(h, 3)].reshape(3 * CH, width))
        value = z[CH : 2 * CH] + from_left(z[:CH]) + from_right(z[2 * CH :])
        act, der = gate(value)
        FI[s, f + 1] = act.astype(BF16)
        D1[at, h] = der

    def cot_rows(k):
        for part in range(2):
            lanes = pl.ds(half * part, half)
            block = to_rows(raw_c.at[k], part)
            CT[0, k % 2, k // 2, lanes, :] = block[0]
            CT[1, k % 2, k // 2, lanes, :] = block[nr - 1]
            CT[pl.ds(2, nr - 2), k % 2, k // 2, lanes, :] = block[1 : nr - 1]

    for f in outer + inner:
        loads_f[f].wait()
        for part in range(2):
            X[place_of[f], pl.ds(1, nr), pl.ds(half * part, half), :] = to_rows(raw_f.at[f], part)
    for f in outer:
        for h in range(1, nr - 1):
            conv_row(place_of[f], f, h, h + 1)

    hear(barrier, 1, True, nbatch - 1)

    used = [0]

    def remote(src, dst, device):
        n = used[0]
        used[0] += 1
        return pltpu.make_async_remote_copy(
            src_ref=src, dst_ref=dst, send_sem=sends.at[n], recv_sem=recvs.at[n],
            device_id=device, device_id_type=MESH,
        )

    class Rows:
        def __init__(self, array, frames):
            self.up = remote(array.at[frames, 1], array.at[frames, nr + 1], above)
            self.down = remote(array.at[frames, nr], array.at[frames, 0], below)

        def start(self):
            pl.when(has_above)(self.up.start)
            pl.when(has_below)(self.down.start)

        def wait(self):
            pl.when(has_above)(self.down.wait_recv)
            pl.when(has_below)(self.up.wait_recv)

        def drain(self):
            pl.when(has_above)(self.up.wait_send)
            pl.when(has_below)(self.down.wait_send)

    class Frames:
        def __init__(self, back_src, back_dst, fore_src, fore_dst):
            self.both = (remote(back_src, back_dst, before), remote(fore_src, fore_dst, after))

        def start(self):
            for copy in self.both:
                copy.start()

        def wait(self):
            for copy in self.both:
                copy.wait_recv()

        def drain(self):
            for copy in self.both:
                copy.wait_send()

    def outer_frames(array, rows):
        return Frames(array.at[rows, 1], array.at[rows, nf + 1], array.at[rows, nf], array.at[rows, 0])

    edges, middle = pl.ds(0, 2), pl.ds(2, nr - 2)
    first_two, second_two = pl.ds(0, 2), pl.ds(2, 2)
    x_outer, x_inner = Rows(X, first_two), Rows(X, second_two)
    first_middle, first_edges = outer_frames(FI, middle), outer_frames(FI, edges)
    cot_far = Frames(cot.at[:, 1], raw_c.at[nf + 3], cot.at[:, nf - 2], raw_c.at[0])
    cot_near = Frames(cot.at[:, 0], raw_c.at[nf + 2], cot.at[:, nf - 1], raw_c.at[1])
    back_middle, back_edges = outer_frames(BS, middle), outer_frames(BS, edges)
    rows_inner, rows_outer = Rows(BF, second_two), Rows(BF, first_two)

    x_outer.start()
    first_middle.start()
    cot_far.start()
    pass_on(0)
    for f in inner:
        for h in range(1, nr - 1):
            conv_row(place_of[f], f, h, h + 1)
    x_inner.start()
    cot_near.start()

    def keep_second(f, s, value):
        act, der = gate(value)
        SE[s, f % 2, f // 2] = act.astype(BF16)
        D2[s, f] = der

    def second_inner(s):
        z = dot(W1F2[...], FI[s, pl.ds(1, 4)].reshape(4 * CH, width))
        keep_second(1, s, z[:CH])
        keep_second(2, s, z[CH:])

    def second_outer(s):
        for f in outer:
            keep_second(f, s, dot(W1F[...], FI[s, pl.ds(f, 3)].reshape(3 * CH, width)))

    def back_second(f, s):
        p, q = f % 2, f // 2
        total = dot(W2B[...], CT[s, p, pl.ds(q, 3)].reshape(3 * CH, width))
        BS[s, f + 1] = (total * D2[s, f]).astype(BF16)

    for s in range(2, nr):
        second_inner(s)
    for f in range(nf):
        loads_c[f].wait()
        cot_rows(f + 2)
    pass_on(1)
    first_middle.wait()
    for s in range(2, nr):
        second_outer(s)

    x_outer.wait()
    for f in outer:
        conv_row(place_of[f], f, 0, 0)
        conv_row(place_of[f], f, nr - 1, 1)
    first_edges.start()

    cot_far.wait()
    cot_rows(0)
    cot_rows(nf + 3)
    for s in range(2, nr):
        for f in outer:
            back_second(f, s)
    back_middle.start()

    pass_on(2)
    x_inner.wait()
    for f in inner:
        conv_row(place_of[f], f, 0, 0)
        conv_row(place_of[f], f, nr - 1, 1)
    for s in range(2):
        second_inner(s)

    first_edges.wait()
    for s in range(2):
        second_outer(s)
        for f in outer:
            back_second(f, s)
    back_edges.start()

    pass_on(3)
    cot_near.wait()
    cot_rows(1)
    cot_rows(nf + 2)
    for s in range(nr):
        for f in inner:
            back_second(f, s)

    def keep_back(f, h, value):
        at = place_of[f]
        value = value * D1[at, h]
        BF[at, h + 1] = value.astype(BF16)
        BFL[at, h] = from_right(value).astype(BF16)
        BFR[at, h] = from_left(value).astype(BF16)

    def back_inner(h, s):
        z = dot(W1B2[...], BS[s, pl.ds(1, 4)].reshape(4 * CH, width))
        keep_back(1, h, z[:CH])
        keep_back(2, h, z[CH:])

    def back_outer(h, s):
        for f in outer:
            keep_back(f, h, dot(W1B[...], BS[s, pl.ds(f, 3)].reshape(3 * CH, width)))

    back_inner(0, 0)
    back_inner(nr - 1, 1)
    rows_inner.start()
    for h in range(1, nr - 1):
        back_inner(h, h + 1)
    back_middle.wait()
    for h in range(1, nr - 1):
        back_outer(h, h + 1)

    low = lax.broadcasted_iota(jnp.int32, (CH, 2 * CH), 1) < CH

    def side_by_side(left, right):
        return jnp.where(low[: left.shape[0]], left, pltpu.roll(right, CH, 1))

    def reduce_scatter(pack, send, recv, which):
        rows = send.shape[1]
        for g in range(nxy):
            send[g] = pack[pl.ds(rows * g, rows), :]
        recv[me] = send[me]

        def one(d, _):
            g = lax.rem(me + d, nxy)
            copy_to(send.at[g], recv.at[me], which, xy_device(g)).start()
            return 0

        lax.fori_loop(1, nxy, one, 0)

    def copy_to(src, dst, which, device):
        return pltpu.make_async_remote_copy(
            src_ref=src, dst_ref=dst, send_sem=ars.at[which], recv_sem=arr.at[which],
            device_id=device, device_id_type=MESH,
        )

    def await_all(ref, count, sem):
        part = ref.at[pl.ds(0, count)]
        pltpu.make_async_copy(part, part, sem).wait()

    def added(ref):
        total = ref[0]
        for g in range(1, ref.shape[0]):
            total += ref[g]
        return total

    def exchange_tm(send, recv, spread, which):
        await_all(recv, nxy - 1, arr.at[which])
        spread[t] = added(recv)

        def one(d, _):
            s = lax.rem(t + d, ntm)
            copy_to(spread.at[t], spread.at[t], which + 1, tm_device(s)).start()
            return 0

        lax.fori_loop(1, ntm, one, 0)

    def gather_xy(spread, gathered, which):
        await_all(spread, ntm - 1, arr.at[which + 1])
        gathered[me] = added(spread)

        def one(d, _):
            g = lax.rem(me + d, nxy)
            copy_to(gathered.at[me], gathered.at[me], which + 2, xy_device(g)).start()
            return 0

        lax.fori_loop(1, nxy, one, 0)

    def unpack(packed, gathered, which):
        await_all(gathered, nxy - 1, arr.at[which + 2])
        rows = gathered.shape[1]
        for g in range(nxy):
            packed[pl.ds(rows * g, rows), :] = gathered[g] * scale

    def lanes_of(parts):
        return jnp.concatenate(parts, axis=1)

    total1 = jnp.zeros((2 * CH, 4 * CH), F32)
    total2 = jnp.zeros((4 * CH, 2 * CH), F32)
    for s in range(0, nr, 2):
        at = [(s, 0), (s, 2), (s + 1, 0), (s + 1, 2)]
        total1 += dot_nt(
            lanes_of([BS[n, pl.ds(f + 1, 2)].reshape(2 * CH, width) for n, f in at]),
            lanes_of([FI[n, pl.ds(f, 4)].reshape(4 * CH, width) for n, f in at]),
        )
        at = [(s, 0), (s, 1), (s + 1, 0), (s + 1, 1)]
        total2 += dot_nt(
            lanes_of([CT[n, p].reshape(4 * CH, width) for n, p in at]),
            lanes_of([SE[n, p].reshape(2 * CH, width) for n, p in at]),
        )
    s1 = total1[:CH] + pltpu.roll(total1[CH:], 3 * CH, 1)
    s2 = total2[: 3 * CH] + pltpu.roll(total2[CH:], CH, 1)
    pack1[pl.ds(0, CH), :] = s1[:, : 2 * CH]
    pack1[pl.ds(CH, CH), :] = side_by_side(s1[:, 2 * CH :], s2[:CH])
    pack1[pl.ds(2 * CH, CH), :] = side_by_side(s2[CH : 2 * CH], s2[2 * CH :])
    pass_on(4)
    reduce_scatter(pack1, a1s, a1r, 0)

    wide = [jnp.zeros((2 * CH, 4 * CH), F32)] * 3

    def versions(at, h, count):
        return (
            BFL[at, pl.ds(h, count)].reshape(count * CH, width),
            BF[at, pl.ds(h + 1, count)].reshape(count * CH, width),
            BFR[at, pl.ds(h, count)].reshape(count * CH, width),
        )

    def spatial(at_list, count):
        lefts = [versions(at, h, count) for at, h in at_list]
        right = lanes_of([X[at, pl.ds(h, count + 2)].reshape((count + 2) * CH, width) for at, h in at_list])
        left = jnp.concatenate([lanes_of([v[j] for v in lefts]) for j in range(3)], axis=0)
        return dot_nt(left, right)

    pairs = spatial([(0, h) for h in range(1, nr - 1, 2)], 2)
    for at in range(1, nf):
        pairs += spatial([(at, h) for h in range(1, nr - 1, 2)], 2)
    for j in range(3):
        total = pairs[2 * CH * j : 2 * CH * j + CH] + pltpu.roll(pairs[2 * CH * j + CH : 2 * CH * (j + 1)], 3 * CH, 1)
        wide[j] = total[:, : 3 * CH]

    back_edges.wait()
    back_outer(0, 0)
    back_outer(nr - 1, 1)
    singles = spatial([(at, h) for at in range(nf) for h in (0, nr - 1)], 1)
    tails = []
    for j in range(3):
        total = wide[j] + singles[CH * j : CH * (j + 1)]
        pack2[pl.ds(CH * j, CH), :] = total[:, : 2 * CH]
        tails.append(jnp.concatenate([total[:, 2 * CH :], total[:, 2 * CH :]], axis=1))
    pack2[pl.ds(3 * CH, CH), :] = jnp.where(low, tails[0], tails[1])
    pack2[pl.ds(4 * CH, half), :] = jnp.where(low[:half], tails[2][:half], tails[2][half:])
    reduce_scatter(pack2, a2s, a2r, 3)
    exchange_tm(a1s, a1r, b1r, 0)

    def grad_row(at, h):
        z = dot(WB[...], BF[at, pl.ds(h, 3)].reshape(3 * CH, width))
        value = z[CH : 2 * CH] + from_right(z[:CH]) + from_left(z[2 * CH :])
        IG[at, h] = value.astype(BF16)

    def hand_out(f):
        at = place_of[f]
        grad_row(at, 0)
        grad_row(at, nr - 1)
        for part in range(2):
            block = IG[at, :, pl.ds(half * part, half), :].reshape(half * nr, width)
            raw_o[pl.ds(half * part, half), f] = dot(POUT[...], block).reshape(half, nr, width).astype(BF16)

    def grad_inner(at, _):
        for h in range(1, nr - 1):
            grad_row(at, h)
        return 0

    lax.fori_loop(0, nf, grad_inner, 0)
    exchange_tm(a2s, a2r, b2r, 3)
    rows_outer.start()
    rows_inner.wait()
    for f in inner:
        hand_out(f)
    gather_xy(b1r, c1r, 0)
    rows_outer.wait()
    for f in outer:
        hand_out(f)
    gather_xy(b2r, c2r, 3)
    unpack(out1, c1r, 0)
    unpack(out2, c2r, 3)
    halos = (x_outer, x_inner, first_middle, first_edges, cot_far, cot_near)
    for halo in halos + (back_middle, back_edges, rows_inner, rows_outer):
        halo.drain()
    for which, sent in ((0, (a1s, b1r, c1r)), (3, (a2s, b2r, c2r))):
        for n, count in enumerate((nxy, ntm, nxy)):
            await_all(sent[n], count - 1, ars.at[which + n])


def per_device(sizes, features, cotangent, w_spatial, w_first, w_second):
    _, ch, nf, nr, width = features.shape
    ntm, nheight, nbatch = sizes
    nxy = nheight * nbatch
    count = nbatch * nf * ntm * nr * nheight * width
    scale = 1.0 / math.sqrt(count)
    vmem = lambda shape, kind=BF16: pltpu.VMEM(shape, kind)
    all1, all2 = 3 * ch, 9 * ch // 2
    rows1, rows2 = all1 // nxy, all2 // nxy
    dma = pltpu.SemaphoreType.DMA
    scratch = [
        vmem((3, 3, ch, ch)), vmem((3, ch, ch)), vmem((3, ch, ch)),
        vmem((nf, ch, nr, width)), vmem((nf + 4, ch, nr, width)),
        vmem((nf, nr + 2, ch, width)),
        vmem((nr, nf + 2, ch, width)),
        vmem((nf, nr, ch, width), F32),
        vmem((nr, nf, ch, width), F32),
        vmem((nr, 2, nf // 2 + 2, ch, width)),
        vmem((nr, 2, nf // 2, ch, width)),
        vmem((nr, nf + 2, ch, width)),
        vmem((nf, nr + 2, ch, width)),
        vmem((nf, nr, ch, width)), vmem((nf, nr, ch, width)), vmem((nf, nr, ch, width)),
        vmem((3 * ch, 3 * ch)), vmem((3 * ch, 3 * ch)),
        vmem((ch, 3 * ch)), vmem((ch, 3 * ch)), vmem((2 * ch, 4 * ch)), vmem((2 * ch, 4 * ch)), vmem((ch, 3 * ch)),
        vmem((ch // 2 * nr, ch // 2 * nr)), vmem((ch // 2 * nr, ch // 2 * nr)),
        vmem((all1, 2 * ch), F32), vmem((all2, 2 * ch), F32),
        vmem((nxy, rows1, 2 * ch), F32), vmem((nxy, rows1, 2 * ch), F32),
        vmem((ntm, rows1, 2 * ch), F32), vmem((nxy, rows1, 2 * ch), F32),
        vmem((nxy, rows2, 2 * ch), F32), vmem((nxy, rows2, 2 * ch), F32),
        vmem((ntm, rows2, 2 * ch), F32), vmem((nxy, rows2, 2 * ch), F32),
        dma((2 * nf + 3,)), dma((20,)), dma((20,)), dma((6,)), dma((6,)), pltpu.SemaphoreType.REGULAR((4,)),
    ]
    here = pl.BlockSpec(memory_space=pltpu.VMEM)
    far = pl.BlockSpec(memory_space=pltpu.HBM)
    block, packed1, packed2 = pl.pallas_call(
        functools.partial(kernel, sizes, scale),
        out_shape=(
            jax.ShapeDtypeStruct((ch, nf, nr, width), BF16),
            jax.ShapeDtypeStruct((all1, 2 * ch), F32),
            jax.ShapeDtypeStruct((all2, 2 * ch), F32),
        ),
        in_specs=[far] * 5,
        out_specs=(here, here, here),
        scratch_shapes=scratch,
        compiler_params=pltpu.CompilerParams(
            collective_id=0, has_side_effects=True, vmem_limit_bytes=48 * 1024 * 1024
        ),
        name="critic_step",
    )(*(pltpu.with_memory_space_constraint(a, pltpu.HBM) for a in (features[0], cotangent[0], w_spatial, w_first, w_second)))
    input_grad, grad_spatial, grad_first, grad_second = pl.pallas_call(
        finish,
        out_shape=(
            jax.ShapeDtypeStruct((ch, nf, nr, width), BF16),
            jax.ShapeDtypeStruct((3, 3, ch, ch), F32),
            jax.ShapeDtypeStruct((3, ch, ch), F32),
            jax.ShapeDtypeStruct((3, ch, ch), F32),
        ),
        in_specs=[here] * 3,
        out_specs=(far, far, far, far),
        scratch_shapes=[
            vmem((3, 3, ch, ch), F32), vmem((3, ch, ch), F32), vmem((3, ch, ch), F32), dma((4,)),
        ],
        compiler_params=pltpu.CompilerParams(vmem_limit_bytes=8 * 1024 * 1024),
        name="hand_out_results",
    )(packed1, packed2, block)
    return input_grad[None], grad_spatial, grad_first, grad_second


def solution(mesh):
    sizes = tuple(mesh.shape[axis] for axis in AXES)
    big = P("batch", None, "tm", "height", None)
    return jax.shard_map(
        functools.partial(per_device, sizes),
        mesh=mesh,
        in_specs=(big, big, P(), P(), P()),
        out_specs=(big, P(), P(), P()),
        check_vma=False,
    )
```
